32 devices in a mesh: occ: 4 (over x, core), vir: 8 (over z, y).
Axes of the slice: x: 2, y: 2, z: 4, core: 2. Of those that a mesh axis runs over, the one named last changes fastest.
Arguments:
- integrals: bfloat16 [16, 3072, 4, 3072], P('occ', 'vir'), may hold values from -0.15625 to 0.15625
- amplitudes: bfloat16 [4, 3072, 2048], P(None, 'vir', 'occ'), may hold values from -6 to 6
- irrep_labels: int32 [3072], replicated, may hold values from 0 to 7, as said below
Outputs:
- ladder: bfloat16 [16, 3072, 2048], P(None, 'vir', 'occ')
The draws below stay inside these ranges and needn't reach their ends.
Inputs may be any that keep to these rules, and one draw needn't show every extreme that they name: `irrep_labels`: every label from 0 to 7 occurs; no label is held by more than 768 orbitals, and one label by exactly that many.
All inputs are finite; a program needn't handle non-finite values.
Results may differ from the reference program's by a relative error of at most 0.001.
Values may be sent and summed in bfloat16 or wider, within the bound.
No kernel may reach another device: no remote copies, remote signals or barrier semaphores. Data moves between devices by JAX's collectives and lax.ppermute only.
A program may use at most 640 MiB of HBM per device.

```python
import jax
import jax.numpy as jnp
from jax import lax

NV = 3072
NIRREP = 8
NA = 16
NC = 4
NP = 2048


def draw_irrep_labels(key, part):
    key = jax.random.fold_in(key, 7)
    key_weights, key_place, key_order = jax.random.split(key, 3)
    weights = jax.random.randint(key_weights, (NIRREP - 1,), 2, 6).astype(jnp.int32)
    largest = NV // 4
    remain = NV - largest
    totals = jnp.cumsum(weights)
    inner_ends = (totals * remain // totals[-1]).astype(jnp.int32)
    small_sizes = jnp.diff(jnp.concatenate([jnp.zeros((1,), jnp.int32), inner_ends]))
    placed = jax.random.randint(key_place, (), 0, NIRREP).astype(jnp.int32)
    labels_all = jnp.arange(NIRREP, dtype=jnp.int32)
    small_index = jnp.clip(labels_all - (labels_all > placed).astype(jnp.int32), 0, NIRREP - 2)
    sizes = jnp.where(labels_all == placed, largest, small_sizes[small_index]).astype(jnp.int32)
    ends = jnp.cumsum(sizes)
    positions = jnp.arange(NV, dtype=jnp.int32)
    sorted_labels = jnp.sum((positions[:, None] >= ends[None, :-1]).astype(jnp.int32), axis=1).astype(jnp.int32)
    order = jax.random.permutation(key_order, NV).astype(jnp.int32)
    return sorted_labels[order].astype(jnp.int32)


def block_levels(rng, shape, shards, low, top_value):
    gain, own = 1.0, jax.random.fold_in(rng, 6)
    for axis_at, blocks in shards:
        steps = jnp.exp(jax.random.uniform(jax.random.fold_in(own, axis_at), (blocks,), jnp.float32, low / len(shards), top_value / len(shards)))
        gain = gain * jnp.repeat(steps, shape[axis_at] // blocks).reshape([-1 if axis == axis_at else 1 for axis in range(len(shape))])
    return gain


def centred(own_key, shape, deviation, most, shards=(), kind=jnp.bfloat16):
    drawn = jax.random.normal(own_key, shape, jnp.float32) * deviation
    if len(shards) > 0:
        drawn = block_levels(own_key, shape, shards, -0.22, 0.18) * drawn
    return jnp.clip(drawn, min=-most, max=most).astype(kind)


def setup_inputs(seed: int = 0) -> dict:
    seeds = jax.random.split(jax.random.key(seed), 4)
    return {
        "integrals": centred(seeds[0], (NA, NV, NC, NV), (NC * NV // 8) ** -0.5, 0.15625, ((0, 4), (1, 8))),
        "amplitudes": centred(seeds[1], (NC, NV, NP), 1.0, 6.0, ((1, 8), (2, 4))),
        "irrep_labels": draw_irrep_labels(jax.random.fold_in(seeds[3], 71), 0),
    }


def reference(integrals, amplitudes, irrep_labels):
    allowed = (irrep_labels[:, None] == irrep_labels[None, :]).astype(jnp.bfloat16)
    flat_amp = amplitudes.reshape(NC * NV, NP)

    def one_row(slab):
        masked = (slab * allowed[:, None, :]).reshape(NV, NC * NV)
        return jnp.dot(masked, flat_amp, preferred_element_type=jnp.float32).astype(jnp.bfloat16)

    return lax.map(one_row, integrals)
```

```python
import functools

import jax
import jax.numpy as jnp
from jax import lax
from jax.experimental import pallas as pl
from jax.experimental.pallas import tpu as pltpu
from jax.sharding import PartitionSpec as P

LABELS = 8
TILE = 128
RUN = 4
TILES = 4
GROUP = RUN * TILES
PIECE = 16
STRIDE = 1024
VMEM = 56 * 2**20
HEAD = ((72, 8), (120, 12))
TAILS = ((216, 24), (240, 24), (272, 24))


def before(values):
    count = values.shape[0]
    earlier = jnp.arange(count)[:, None] > jnp.arange(count)[None, :]
    earlier = earlier.reshape(earlier.shape + (1,) * (values.ndim - 1))
    return jnp.sum(jnp.where(earlier, values[None], 0), axis=1)


def make_plan(labels, rows, vir, shard, tails):
    total = labels.shape[0]
    blocks = total // TILE
    names = jnp.arange(LABELS)
    member = labels.reshape(1, blocks, TILE) == names[:, None, None]
    lower = jnp.arange(TILE)[:, None] < jnp.arange(TILE)[None, :]
    within = jnp.dot(
        member.astype(jnp.bfloat16).reshape(LABELS * blocks, TILE),
        lower.astype(jnp.bfloat16),
        preferred_element_type=jnp.float32,
    )
    within = within.reshape(LABELS, blocks, TILE).astype(jnp.int32)
    held = jnp.sum(member.astype(jnp.int32), axis=2)
    held_before = before(held.T).T
    rank = jnp.sum(jnp.where(member, within + held_before[:, :, None], 0), axis=0).reshape(total)
    sizes = jnp.sum(held, axis=1)
    depth = (sizes + TILE - 1) // TILE

    shards = total // shard
    part = jnp.sum(held.reshape(LABELS, shards, shard // TILE), axis=2)
    part_before = before(part.T).T
    pieces = jnp.where(part > 0, (part_before % PIECE + part + PIECE - 1) // PIECE, 0)
    piece_from = before(pieces)
    piece_to = part_before // PIECE
    move = PIECE * (piece_from - piece_to)
    slot = rank.reshape(shards, shard) + jnp.sum(
        jnp.where(member.reshape(LABELS, shards, shard), move[:, :, None], 0), axis=0
    )

    slices = total // rows
    mine = labels.reshape(1, slices, rows) == names[:, None, None]
    count = jnp.sum(mine.astype(jnp.int32), axis=2)
    row_tiles = (count + RUN - 1) // RUN
    groups = (count + GROUP - 1) // GROUP
    group_from = before(groups)
    unit_from = before(row_tiles * depth[:, None])
    most = rows // GROUP + LABELS + 1
    at = jnp.arange(most)[None, :, None]
    inside = (at >= group_from[:, None]) & (at < (group_from + groups)[:, None])

    def pick(values):
        return jnp.sum(jnp.where(inside, values, 0), axis=0)

    order = jnp.where(inside, at - group_from[:, None], 0)
    group_tiles = pick(jnp.clip(row_tiles[:, None] - TILES * order, 0, TILES))
    group_depth = pick(depth[:, None, None])
    group_unit = pick(unit_from[:, None] + order * TILES * depth[:, None, None])
    group_label = pick(names[:, None, None])
    group_end = group_unit + group_tiles * group_depth
    live = jnp.sum(groups, axis=0)
    valid = jnp.arange(most)[:, None] < live[None]
    starts, bases = [jnp.zeros_like(live)], [jnp.zeros_like(live)]
    for size, steps in HEAD:
        fits = valid & (group_end <= (bases[-1] + size)[None])
        fits = fits & (jnp.arange(most)[:, None] < (starts[-1] + steps)[None])
        starts.append(jnp.sum(fits.astype(jnp.int32), axis=0))
        bases.append(jnp.max(jnp.where(fits, group_end, 0), axis=0))
    rest = jnp.max(jnp.sum(row_tiles * depth[:, None], axis=0) - bases[-1])
    left = jnp.max(live - starts[-1])
    variant = sum(((rest > size) | (left > steps)).astype(jnp.int32) for size, steps in tails)
    starts.append(live)
    starts, bases = jnp.stack(starts), jnp.stack(bases)
    chunk = jnp.sum((jnp.arange(most)[:, None, None] >= starts[None, 1:-1]).astype(jnp.int32), axis=1)
    base = jnp.sum(
        jnp.where(chunk[None] == jnp.arange(len(HEAD) + 1)[:, None, None], bases[:, None], 0), axis=0
    )

    def own(values):
        return lax.dynamic_index_in_dim(values, vir, axis=values.ndim - 1, keepdims=False)

    group_from, count_before = own(group_from), own(before(count.T).T)
    row_label = lax.dynamic_slice_in_dim(labels, vir * rows, rows, 0)
    row_rank = lax.dynamic_slice_in_dim(rank, vir * rows, rows, 0)
    row_member = row_label[None, :] == names[:, None]
    row_slot = row_rank + jnp.sum(
        jnp.where(row_member, (GROUP * group_from - count_before)[:, None], 0), axis=0
    )
    hit = jnp.arange(most * GROUP)[:, None] == row_slot[None, :]
    orbital = jnp.sum(jnp.where(hit, jnp.arange(rows)[None, :] + 1, 0), axis=1) - 1
    return dict(
        key=(labels * STRIDE + rank).reshape(1, total),
        pieces=pieces.reshape(-1),
        piece_from=piece_from.reshape(-1),
        piece_to=piece_to.reshape(-1),
        slot=slot.reshape(shards, 1, shard),
        label=own(group_label),
        tiles=own(group_tiles),
        depth=own(group_depth),
        unit=own(group_unit - base),
        starts=own(starts),
        orbital=orbital.reshape(1, most * GROUP),
        variant=variant,
    )


def place_of(span, step, spare):
    return jnp.where(span[1] > span[0], jnp.minimum(span[0] + step, span[1] - 1), spare)


def compact_kernel(span, label, unit, tiles, depth, orbital, key_ref, *refs):
    slabs = refs[:GROUP]
    out_ref, onehot, held, product, stage, sem = refs[GROUP:]
    step = pl.program_id(0)
    last = pl.num_programs(0) - 1
    i = place_of(span, step, label.shape[0] - 1)
    na, _, nc, width = slabs[0].shape
    rows = na * nc
    slot = lax.rem(step, 2)
    deep, name = depth[i], label[i]

    def active(step):
        return span[0] + step < span[1]

    @pl.when(active(step) & ((step == 0) | (label[jnp.maximum(i - 1, 0)] != name)))
    def _():
        def build(k, carry):
            place = lax.broadcasted_iota(jnp.int32, (2 * TILE, width), 0)
            place = place + (name * STRIDE + k * 2 * TILE)
            onehot[k] = (key_ref[...] == place).astype(jnp.float32).astype(jnp.bfloat16)
            return carry

        lax.fori_loop(0, (deep + 1) // 2, build, 0)

    def copy(step, s):
        j = place_of(span, step, label.shape[0] - 1)
        size = tiles[j] * depth[j]
        return pltpu.make_async_copy(
            stage.at[s, pl.ds(0, size)], out_ref.at[pl.ds(unit[j], size)], sem.at[s]
        )

    @pl.when((step >= 2) & active(step - 2))
    def _():
        copy(step - 2, slot).wait()

    @pl.when(active(step))
    def _():
        for r in range(GROUP):
            held[r * rows : (r + 1) * rows, :] = slabs[r][...].reshape(rows, width)

        def part(k, carry):
            full = lax.dot_general(
                held[...], onehot[k], (((1,), (1,)), ((), ())), preferred_element_type=jnp.float32
            )
            for h in range(2):
                product[h] = full[:, h * TILE : (h + 1) * TILE]
            for h in range(2):

                @pl.when(2 * k + h < deep)
                def _():
                    for c in range(nc):
                        one = product[h, pl.ds(c, GROUP * na, stride=nc), :].astype(jnp.bfloat16)
                        for r in range(TILES):
                            stage[slot, r * deep + 2 * k + h, c] = one[
                                r * RUN * na : (r + 1) * RUN * na
                            ]

            return carry

        lax.fori_loop(0, (deep + 1) // 2, part, 0)
        copy(step, slot).start()

    @pl.when((step == last) & (step >= 1) & active(step - 1))
    def _():
        copy(step - 1, 1 - slot).wait()

    @pl.when((step == last) & active(step))
    def _():
        copy(step, slot).wait()


def compact(integrals, plan, chunk, size, steps, pairs):
    na, rows, nc, width = integrals.shape
    spare = plan["label"].shape[0] - 1

    def slab(r):
        def at(step, span, label, unit, tiles, depth, orbital):
            return 0, orbital[place_of(span, step, spare) * GROUP + r], 0, 0

        return pl.BlockSpec((na, 1, nc, width), at)

    return pl.pallas_call(
        compact_kernel,
        grid_spec=pltpu.PrefetchScalarGridSpec(
            num_scalar_prefetch=6,
            grid=(steps,),
            in_specs=[pl.BlockSpec((1, width), lambda step, *_: (0, 0))]
            + [slab(r) for r in range(GROUP)],
            out_specs=pl.BlockSpec(memory_space=pl.ANY),
            scratch_shapes=[
                pltpu.VMEM((pairs, 2 * TILE, width), jnp.bfloat16),
                pltpu.VMEM((GROUP * na * nc, width), jnp.bfloat16),
                pltpu.VMEM((2, GROUP * na * nc, TILE), jnp.float32),
                pltpu.VMEM((2, TILES * 2 * pairs, nc, RUN * na, TILE), jnp.bfloat16),
                pltpu.SemaphoreType.DMA((2,)),
            ],
        ),
        out_shape=jax.ShapeDtypeStruct((size, nc, RUN * na, TILE), jnp.bfloat16),
        compiler_params=pltpu.CompilerParams(vmem_limit_bytes=VMEM),
        cost_estimate=pl.CostEstimate(
            flops=size * 2 * 10**8, bytes_accessed=integrals.size, transcendentals=0
        ),
        name="compact",
    )(
        plan["starts"][chunk : chunk + 2], plan["label"], plan["unit"], plan["tiles"], plan["depth"],
        jnp.maximum(plan["orbital"].reshape(-1), 0), plan["key"], *([integrals] * GROUP),
    )


def sort_kernel(slots, nbuf, source, row, pieces, piece_from, piece_to, slot_ref, *refs):
    buffers = refs[:nbuf]
    out_ref, onehot, held, moved, sem = refs[nbuf:]
    c, v = pl.program_id(0), pl.program_id(1)
    shards = pl.num_programs(1)
    steps = pl.num_programs(0) * shards
    step = c * shards + v
    width = held.shape[1]

    def fetch(step, start):
        c, v, s = step // shards, lax.rem(step, shards), lax.rem(step, 2)
        for at in range(nbuf):

            @pl.when(source[v] == at)
            def _():
                copy = pltpu.make_async_copy(
                    buffers[at].at[c, pl.ds(pl.multiple_of(row[v], width), width)], held.at[s], sem.at[s]
                )
                if start:
                    copy.start()
                else:
                    copy.wait()

    @pl.when(step == 0)
    def _():
        fetch(step, True)

    @pl.when(step + 1 < steps)
    def _():
        fetch(step + 1, True)

    @pl.when(c == 0)
    def _():
        place = lax.broadcasted_iota(jnp.int32, (slots, width), 0)
        onehot[v] = (slot_ref[...].reshape(1, width) == place).astype(jnp.float32).astype(jnp.bfloat16)

    @pl.when(v == 0)
    def _():
        out_ref[...] = jnp.zeros_like(out_ref)

    fetch(step, False)
    sorted_rows = jnp.dot(onehot[v], held[lax.rem(step, 2)], preferred_element_type=jnp.float32)
    moved[...] = sorted_rows.astype(jnp.bfloat16).reshape(moved.shape)
    per_tile = TILE // PIECE
    for g in range(LABELS):
        at = g * shards + v
        source_piece, target_piece = piece_from[at], piece_to[at]

        def add(i, carry):
            target = target_piece + i
            tile, place = target // per_tile, lax.rem(target, per_tile)
            out_ref[g, tile, 0, place] = out_ref[g, tile, 0, place] + moved[source_piece + i]
            return carry

        lax.fori_loop(0, pieces[at], add, 0)


def sort_amplitudes(buffers, source, row, plan, deepest):
    nc, _, pairs = buffers[0].shape
    shards, _, shard = plan["slot"].shape
    slots = -(-(shard + LABELS * 2 * (PIECE - 1)) // TILE) * TILE
    return pl.pallas_call(
        functools.partial(sort_kernel, slots, len(buffers)),
        grid_spec=pltpu.PrefetchScalarGridSpec(
            num_scalar_prefetch=5,
            grid=(nc, shards),
            in_specs=[pl.BlockSpec((1, 1, shard), lambda c, v, *_: (v, 0, 0))]
            + [pl.BlockSpec(memory_space=pl.ANY)] * len(buffers),
            out_specs=pl.BlockSpec(
                (LABELS, deepest, 1, TILE // PIECE, PIECE, pairs), lambda c, v, *_: (0, 0, c, 0, 0, 0)
            ),
            scratch_shapes=[
                pltpu.VMEM((shards, slots, shard), jnp.bfloat16),
                pltpu.VMEM((2, shard, pairs), jnp.bfloat16),
                pltpu.VMEM((slots // PIECE, PIECE, pairs), jnp.bfloat16),
                pltpu.SemaphoreType.DMA((2,)),
            ],
        ),
        out_shape=jax.ShapeDtypeStruct(
            (LABELS, deepest, nc, TILE // PIECE, PIECE, pairs), jnp.bfloat16
        ),
        compiler_params=pltpu.CompilerParams(vmem_limit_bytes=VMEM),
        cost_estimate=pl.CostEstimate(
            flops=2 * slots * shards * shard * nc * pairs, bytes_accessed=5 * 10**7, transcendentals=0
        ),
        name="sort_amplitudes",
    )(source, row, plan["pieces"], plan["piece_from"], plan["piece_to"], plan["slot"], *buffers)


def multiply_kernel(cap, window, span, label, unit, tiles, depth, origin, *refs):
    sources, amp_ref = refs[:4], refs[4]
    out_ref, total_ref = refs[-2:]
    step = pl.program_id(0)
    i = place_of(span, step, label.shape[0] - 1)
    _, nc, rows, _ = sources[0].shape
    na = rows // RUN
    columns = amp_ref.shape[-1] // TILE
    count, deep = tiles[i], depth[i]
    shift = unit[i] - jnp.minimum(unit[i], cap - window)

    def left(k):
        parts = []
        for s in range(4):
            for r in range(TILES):
                at = jnp.minimum(shift + jnp.minimum(r, count - 1) * deep + k, window - 1)
                parts.append(jnp.concatenate([sources[s][at, c] for c in range(nc)], axis=1))
        return jnp.concatenate(parts, axis=0)

    for known in range(1, amp_ref.shape[1] + 1):

        @pl.when((span[0] + step < span[1]) & (deep == known))
        def _():
            total = None
            for k in range(known):
                term = jnp.dot(left(k), amp_ref[0, k], preferred_element_type=jnp.float32)
                total = term if total is None else total + term
            for j in range(columns):
                total_ref[j] = total[:, j * TILE : (j + 1) * TILE]
            for s in range(4):
                for a in range(na):
                    for j in range(columns):
                        picked = total_ref[j, pl.ds(s * TILES * rows + a, GROUP, stride=na), :]
                        out_ref[(origin[0] ^ s) * na + a, 0, :, j * TILE : (j + 1) * TILE] = (
                            picked.astype(jnp.bfloat16)
                        )


def multiply(sources, amplitudes, plan, origin, chunk, steps, done):
    cap, nc, rows, _ = sources[0].shape
    deepest, pairs = amplitudes.shape[1], amplitudes.shape[-1]
    na = rows // RUN
    window = TILES * deepest
    most = plan["label"].shape[0]
    spare = most - 1

    def units(step, span, label, unit, *_):
        return jnp.minimum(unit[place_of(span, step, spare)], cap - window), 0, 0, 0

    lanes = pl.BlockSpec(
        (pl.Element(window), pl.Element(nc), pl.Element(rows), pl.Element(TILE)), units
    )
    amp_spec = pl.BlockSpec(
        (1, deepest, nc * TILE, pairs), lambda step, span, label, *_: (label[place_of(span, step, spare)], 0, 0, 0)
    )
    out_spec = pl.BlockSpec(
        (4 * na, 1, GROUP, pairs), lambda step, span, *_: (0, place_of(span, step, spare), 0, 0)
    )
    extra = [] if done is None else [done]
    return pl.pallas_call(
        functools.partial(multiply_kernel, cap, window),
        grid_spec=pltpu.PrefetchScalarGridSpec(
            num_scalar_prefetch=6,
            grid=(steps,),
            in_specs=[lanes] * 4 + [amp_spec] + [pl.BlockSpec(memory_space=pl.ANY)] * len(extra),
            out_specs=out_spec,
            scratch_shapes=[pltpu.VMEM((pairs // TILE, 4 * TILES * rows, TILE), jnp.float32)],
        ),
        out_shape=jax.ShapeDtypeStruct((4 * na, most, GROUP, pairs), jnp.bfloat16),
        input_output_aliases={11: 0} if extra else {},
        compiler_params=pltpu.CompilerParams(vmem_limit_bytes=VMEM),
        cost_estimate=pl.CostEstimate(
            flops=cap * 5 * 10**7, bytes_accessed=cap * 10**5, transcendentals=0
        ),
        name="multiply",
    )(
        plan["starts"][chunk : chunk + 2], plan["label"], plan["unit"], plan["tiles"], plan["depth"], origin,
        *sources, amplitudes.reshape(LABELS, deepest, nc * TILE, pairs), *extra,
    )


def restore_kernel(live, orbital_ref, in_ref, out_ref, onehot, held):
    slots = orbital_ref.shape[1]
    rows, pairs = out_ref.shape[1:]

    @pl.when(pl.program_id(0) == 0)
    def _():
        place = lax.broadcasted_iota(jnp.int32, (rows, slots), 0)
        onehot[...] = (orbital_ref[...] == place).astype(jnp.float32).astype(jnp.bfloat16)

    for g in range(in_ref.shape[1]):
        held[g] = jnp.where(g < live[0], in_ref[0, g], jnp.zeros_like(in_ref[0, g]))
    out_ref[0] = jnp.dot(
        onehot[...], held[...].reshape(slots, pairs), preferred_element_type=jnp.float32
    ).astype(jnp.bfloat16)


def restore(grouped, plan, rows):
    block_a, most, _, pairs = grouped.shape
    return pl.pallas_call(
        restore_kernel,
        grid_spec=pltpu.PrefetchScalarGridSpec(
            num_scalar_prefetch=1,
            grid=(block_a,),
            in_specs=[
                pl.BlockSpec((1, most * GROUP), lambda a, *_: (0, 0)),
                pl.BlockSpec((1, most, GROUP, pairs), lambda a, *_: (a, 0, 0, 0)),
            ],
            out_specs=pl.BlockSpec((1, rows, pairs), lambda a, *_: (a, 0, 0)),
            scratch_shapes=[
                pltpu.VMEM((rows, most * GROUP), jnp.bfloat16),
                pltpu.VMEM((most, GROUP, pairs), jnp.bfloat16),
            ],
        ),
        out_shape=jax.ShapeDtypeStruct((block_a, rows, pairs), jnp.bfloat16),
        compiler_params=pltpu.CompilerParams(vmem_limit_bytes=VMEM),
        cost_estimate=pl.CostEstimate(flops=6 * 10**9, bytes_accessed=15 * 10**6, transcendentals=0),
        name="restore",
    )(plan["starts"][-1:], plan["orbital"], grouped)


def gather_amplitudes(amplitudes, vir, vir_count):
    width = amplitudes.shape[1]
    total = width * vir_count
    if vir_count != 8:
        shard = total // 8
        whole = lax.all_gather(amplitudes, "vir", axis=1, tiled=True)
        return [whole], jnp.zeros((8,), jnp.int32), jnp.arange(8, dtype=jnp.int32) * shard
    lines = vir_count // 2
    buffers = [amplitudes]
    other = [lax.ppermute(amplitudes, "vir", [(i, i ^ 1) for i in range(vir_count)])]
    up = down = amplitudes
    ups, downs, other_ups, other_downs = [], [], [], []
    for k in range(lines - 1):
        up = lax.ppermute(up, "vir", [(i, i + 2) for i in range(2 * k, vir_count - 2)])
        down = lax.ppermute(down, "vir", [(i, i - 2) for i in range(2, vir_count - 2 * k)])
        ups.append(up)
        downs.append(down)
        other_ups.append(
            lax.ppermute(up, "vir", [(i, i ^ 1) for i in range(2 * k + 2, vir_count)])
        )
        other_downs.append(
            lax.ppermute(down, "vir", [(i, i ^ 1) for i in range(0, vir_count - 2 * k - 2)])
        )
    buffers = buffers + ups + downs + other + other_ups + other_downs
    shards = jnp.arange(vir_count, dtype=jnp.int32)
    ahead = shards // 2 - vir // 2
    source = jnp.where(ahead == 0, 0, jnp.where(ahead < 0, -ahead, lines - 1 + ahead))
    source = source + jnp.where(shards % 2 == vir % 2, 0, 2 * lines - 1)
    return buffers, source.astype(jnp.int32), jnp.zeros((vir_count,), jnp.int32)


def on_device(vir_count, integrals, amplitudes, irrep_labels):
    rows = integrals.shape[1]
    total = irrep_labels.shape[0]
    deepest = -(-(total // 4) // TILE)
    vir, occ = lax.axis_index("vir"), lax.axis_index("occ")
    plan = make_plan(irrep_labels, rows, vir, total // 8, TAILS)
    most = ((rows // RUN + LABELS) * deepest, rows // GROUP + LABELS)
    origin = occ.astype(jnp.int32).reshape(1)
    core = [(i, i ^ 1) for i in range(4)]
    chip = [(i, i ^ 2) for i in range(4)]

    def run(sizes, integrals, amplitudes, plan):
        buffers, source, row = gather_amplitudes(amplitudes, vir, vir_count)
        chunks = []
        for at, (size, steps) in enumerate(sizes):
            mine = compact(integrals, plan, at, size, steps, -(-deepest // 2))
            far = lax.ppermute(mine, "occ", chip)
            near = lax.ppermute(mine, "occ", core)
            chunks.append((mine, near, far, lax.ppermute(far, "occ", core)))
        ordered = sort_amplitudes(buffers, source, row, plan, deepest)
        done = None
        for at, sources in enumerate(chunks):
            done = multiply(sources, ordered, plan, origin, at, sizes[at][1], done)
        return restore(done, plan, rows)

    branches = [
        functools.partial(run, HEAD + (tail,)) for tail in TAILS + (most,)
    ]
    return lax.switch(plan["variant"], branches, integrals, amplitudes, plan)


def solution(mesh):
    in_specs = (P("occ", "vir", None, None), P(None, "vir", "occ"), P())
    out_specs = P(None, "vir", "occ")
    return jax.shard_map(
        functools.partial(on_device, mesh.shape["vir"]),
        mesh=mesh, in_specs=in_specs, out_specs=out_specs, check_vma=False,
    )
```

```python
import copy
import functools

import jax
import jax.numpy as jnp
from jax import lax
from jax.experimental import pallas as pl
from jax.experimental.pallas import tpu as pltpu
from jax.sharding import PartitionSpec as P

LABELS = 8
TILE = 128
RUN = 4
TILES = 4
GROUP = RUN * TILES
PIECE = 16
STRIDE = 1024
VMEM = 56 * 2**20
COST = pl.CostEstimate(flops=10**6, bytes_accessed=10**6, transcendentals=0)
HEAD = ((56, 6), (128, 12), (128, 12))
TAILS = ((112, 14), (136, 16), (168, 20))


def before(values):
    count = values.shape[0]
    earlier = jnp.arange(count)[:, None] > jnp.arange(count)[None, :]
    earlier = earlier.reshape(earlier.shape + (1,) * (values.ndim - 1))
    return jnp.sum(jnp.where(earlier, values[None], 0), axis=1)


def slots_of(shard):
    return -(-(shard + LABELS * 2 * (PIECE - 1)) // TILE) * TILE


def make_plan(labels, rows, vir, shard, tails):
    total = labels.shape[0]
    blocks = total // TILE
    names = jnp.arange(LABELS)
    member = labels.reshape(1, blocks, TILE) == names[:, None, None]
    lower = jnp.arange(TILE)[:, None] < jnp.arange(TILE)[None, :]
    within = jnp.dot(
        member.astype(jnp.bfloat16).reshape(LABELS * blocks, TILE),
        lower.astype(jnp.bfloat16),
        preferred_element_type=jnp.float32,
    )
    within = within.reshape(LABELS, blocks, TILE).astype(jnp.int32)
    held = jnp.sum(member.astype(jnp.int32), axis=2)
    held_before = before(held.T).T
    rank = jnp.sum(jnp.where(member, within + held_before[:, :, None], 0), axis=0).reshape(total)
    sizes = jnp.sum(held, axis=1)
    depth = (sizes + TILE - 1) // TILE

    shards = total // shard
    part = jnp.sum(held.reshape(LABELS, shards, shard // TILE), axis=2)
    part_before = before(part.T).T
    pieces = jnp.where(part > 0, (part_before % PIECE + part + PIECE - 1) // PIECE, 0)
    piece_from = before(pieces)
    piece_to = part_before // PIECE
    move = PIECE * (piece_from - piece_to)
    slots = slots_of(shard) // PIECE
    spot = jnp.arange(slots)[None, None]
    taken = (spot >= piece_from[:, :, None]) & (spot < (piece_from + pieces)[:, :, None])
    most_pieces = -(-(total // 4) // TILE) * (TILE // PIECE)
    goal = names[:, None, None] * most_pieces + spot + (piece_to - piece_from)[:, :, None]
    goal = jnp.sum(jnp.where(taken, goal - LABELS * most_pieces, 0), axis=0) + LABELS * most_pieces
    slot = rank.reshape(shards, shard) + jnp.sum(
        jnp.where(member.reshape(LABELS, shards, shard), move[:, :, None], 0), axis=0
    )

    slices = total // rows
    mine = labels.reshape(1, slices, rows) == names[:, None, None]
    count = jnp.sum(mine.astype(jnp.int32), axis=2)
    row_tiles = (count + RUN - 1) // RUN
    groups = (count + GROUP - 1) // GROUP
    group_from = before(groups)
    unit_from = before(row_tiles * depth[:, None])
    most = rows // GROUP + LABELS + 1
    at = jnp.arange(most)[None, :, None]
    inside = (at >= group_from[:, None]) & (at < (group_from + groups)[:, None])

    def pick(values):
        return jnp.sum(jnp.where(inside, values, 0), axis=0)

    order = jnp.where(inside, at - group_from[:, None], 0)
    group_tiles = pick(jnp.clip(row_tiles[:, None] - TILES * order, 0, TILES))
    group_depth = pick(depth[:, None, None])
    group_unit = pick(unit_from[:, None] + order * TILES * depth[:, None, None])
    group_label = pick(names[:, None, None])
    label_end = pick((group_from + groups)[:, None])
    label_turn = pick(jnp.cumsum((groups > 0).astype(jnp.int32), axis=0)[:, None])
    group_end = group_unit + group_tiles * group_depth
    live = jnp.sum(groups, axis=0)
    valid = jnp.arange(most)[:, None] < live[None]
    starts, bases = [jnp.zeros_like(live)], [jnp.zeros_like(live)]
    for size, steps in HEAD:
        fits = valid & (group_end <= (bases[-1] + size)[None])
        fits = fits & (jnp.arange(most)[:, None] < (starts[-1] + steps)[None])
        starts.append(jnp.sum(fits.astype(jnp.int32), axis=0))
        bases.append(jnp.max(jnp.where(fits, group_end, 0), axis=0))
    rest = jnp.max(jnp.sum(row_tiles * depth[:, None], axis=0) - bases[-1])
    left = jnp.max(live - starts[-1])
    variant = sum(((rest > size) | (left > steps)).astype(jnp.int32) for size, steps in tails)
    starts.append(live)
    starts, bases = jnp.stack(starts), jnp.stack(bases)
    chunk = jnp.sum((jnp.arange(most)[:, None, None] >= starts[None, 1:-1]).astype(jnp.int32), axis=1)
    base = jnp.sum(
        jnp.where(chunk[None] == jnp.arange(len(HEAD) + 1)[:, None, None], bases[:, None], 0), axis=0
    )

    def own(values):
        return lax.dynamic_index_in_dim(values, vir, axis=values.ndim - 1, keepdims=False)

    group_from, count_before = own(group_from), own(before(count.T).T)
    row_label = lax.dynamic_slice_in_dim(labels, vir * rows, rows, 0)
    row_rank = lax.dynamic_slice_in_dim(rank, vir * rows, rows, 0)
    row_member = row_label[None, :] == names[:, None]
    row_slot = row_rank + jnp.sum(
        jnp.where(row_member, (GROUP * group_from - count_before)[:, None], 0), axis=0
    )
    hit = jnp.arange(most * GROUP)[:, None] == row_slot[None, :]
    orbital = jnp.sum(jnp.where(hit, jnp.arange(rows)[None, :] + 1, 0), axis=1) - 1
    return dict(
        key=(labels * STRIDE + rank).reshape(1, total),
        pieces=pieces,
        piece_from=piece_from,
        piece_to=piece_to,
        goal=goal,
        slot=slot.reshape(shards, 1, shard),
        label=own(group_label),
        tiles=own(group_tiles),
        depth=own(group_depth),
        unit=own(group_unit - base),
        chunk=own(chunk),
        label_end=own(label_end),
        label_turn=own(label_turn),
        starts=own(starts),
        orbital=orbital.reshape(1, most * GROUP),
        variant=variant,
    )


def place_of(span, step, spare):
    return jnp.where(span[1] > span[0], jnp.minimum(span[0] + step, span[1] - 1), spare)


def compact_kernel(span, label, unit, tiles, depth, orbital, key_ref, *refs):
    slabs = refs[:GROUP]
    out_ref, onehot, held, product, stage, sem = refs[-6:]
    step = pl.program_id(0)
    last = pl.num_programs(0) - 1
    i = place_of(span, step, label.shape[0] - 1)
    na, _, nc, width = slabs[0].shape
    rows = na * nc
    slot = lax.rem(step, 2)
    deep, name = depth[i], label[i]

    def active(step):
        return span[0] + step < span[1]

    @pl.when(active(step) & ((step == 0) | (label[jnp.maximum(i - 1, 0)] != name)))
    def _():
        def build(k, carry):
            place = lax.broadcasted_iota(jnp.int32, (2 * TILE, width), 0)
            place = place + (name * STRIDE + k * 2 * TILE)
            onehot[k] = (key_ref[...] == place).astype(jnp.float32).astype(jnp.bfloat16)
            return carry

        lax.fori_loop(0, (deep + 1) // 2, build, 0)

    def copy(step, s):
        j = place_of(span, step, label.shape[0] - 1)
        size = tiles[j] * depth[j]
        return pltpu.make_async_copy(
            stage.at[s, pl.ds(0, size)], out_ref.at[pl.ds(unit[j], size)], sem.at[s]
        )

    @pl.when((step >= 2) & active(step - 2))
    def _():
        copy(step - 2, slot).wait()

    @pl.when(active(step))
    def _():
        for r in range(GROUP):
            held[r * rows : (r + 1) * rows, :] = slabs[r][...].reshape(rows, width)

        def part(k, carry):
            full = lax.dot_general(
                held[...], onehot[k], (((1,), (1,)), ((), ())), preferred_element_type=jnp.float32
            )
            for h in range(2):
                product[h] = full[:, h * TILE : (h + 1) * TILE]
            for h in range(2):

                @pl.when(2 * k + h < deep)
                def _():
                    for c in range(nc):
                        one = product[h, pl.ds(c, GROUP * na, stride=nc), :].astype(jnp.bfloat16)
                        for r in range(TILES):
                            stage[slot, r * deep + 2 * k + h, c] = one[
                                r * RUN * na : (r + 1) * RUN * na
                            ]

            return carry

        lax.fori_loop(0, (deep + 1) // 2, part, 0)
        copy(step, slot).start()

    @pl.when((step == last) & (step >= 1) & active(step - 1))
    def _():
        copy(step - 1, 1 - slot).wait()

    @pl.when((step == last) & active(step))
    def _():
        copy(step, slot).wait()


def token(*arrays):
    def kernel(*refs):
        refs[-1][...] = jnp.zeros_like(refs[-1])

    return pl.pallas_call(
        kernel,
        in_specs=[pl.BlockSpec(memory_space=pl.ANY)] * len(arrays),
        out_shape=jax.ShapeDtypeStruct((8, TILE), jnp.float32),
        cost_estimate=COST,
        name="token",
    )(*arrays)


def after(array, mark):
    def kernel(*refs):
        del refs

    return pl.pallas_call(
        kernel,
        in_specs=[pl.BlockSpec(memory_space=pl.ANY)] * 2,
        out_specs=pl.BlockSpec(memory_space=pl.ANY),
        out_shape=jax.ShapeDtypeStruct(array.shape, array.dtype),
        input_output_aliases={0: 0},
        cost_estimate=COST,
        name="after",
    )(array, mark)


def compact(integrals, plan, chunk, size, steps, pairs, first):
    na, rows, nc, width = integrals.shape
    spare = plan["label"].shape[0] - 1

    def slab(r):
        def at(step, span, label, unit, tiles, depth, orbital):
            return 0, orbital[place_of(span, step, spare) * GROUP + r], 0, 0

        return pl.BlockSpec((na, 1, nc, width), at)

    return pl.pallas_call(
        compact_kernel,
        grid_spec=pltpu.PrefetchScalarGridSpec(
            num_scalar_prefetch=6,
            grid=(steps,),
            in_specs=[pl.BlockSpec((1, width), lambda step, *_: (0, 0))]
            + [slab(r) for r in range(GROUP)]
            + [pl.BlockSpec(memory_space=pl.ANY)] * len(first),
            out_specs=pl.BlockSpec(memory_space=pl.ANY),
            scratch_shapes=[
                pltpu.VMEM((pairs, 2 * TILE, width), jnp.bfloat16),
                pltpu.VMEM((GROUP * na * nc, width), jnp.bfloat16),
                pltpu.VMEM((2, GROUP * na * nc, TILE), jnp.float32),
                pltpu.VMEM((2, TILES * 2 * pairs, nc, RUN * na, TILE), jnp.bfloat16),
                pltpu.SemaphoreType.DMA((2,)),
            ],
        ),
        out_shape=jax.ShapeDtypeStruct((size, nc, RUN * na, TILE), jnp.bfloat16),
        compiler_params=pltpu.CompilerParams(vmem_limit_bytes=VMEM),
        cost_estimate=COST,
        name="compact",
    )(
        plan["starts"][chunk : chunk + 2], plan["label"], plan["unit"], plan["tiles"], plan["depth"],
        jnp.maximum(plan["orbital"].reshape(-1), 0), plan["key"], *([integrals] * GROUP), *first,
    )


def fetch(buffers, source, row, v, c, held, sem, start):
    width = held.shape[0]
    for at in range(len(buffers)):

        @pl.when(source[v] == at)
        def _():
            rows = pl.ds(pl.multiple_of(row[v], width), width)
            copy = pltpu.make_async_copy(buffers[at].at[c, rows], held, sem)
            if start:
                copy.start()
            else:
                copy.wait()


def selection(slot, slots):
    width = slot.shape[-1]
    place = lax.broadcasted_iota(jnp.int32, (slots, width), 0)
    return (slot.reshape(1, width) == place).astype(jnp.float32).astype(jnp.bfloat16)


def add_kernel(nbuf, low, order, source, row, pieces, piece_from, piece_to, slot_ref, *refs):
    buffers = refs[:nbuf]
    out_ref, held, old, moved, sem, in_sem, out_sem = refs[-7:]
    shards = order.shape[0]
    step = pl.program_id(0)
    steps = pl.num_programs(0)
    nc = old.shape[0]
    slots = old.shape[1] * PIECE
    s = lax.rem(step, 2)

    def get(step, start):
        for c in range(nc):
            h = lax.rem(step, 2)
            fetch(buffers, source, row, order[low + step], c, held.at[h, c], sem.at[h, c], start)

    def each(v, c, do):
        for g in range(LABELS):
            size = pieces[g * shards + v]
            here = old.at[c, pl.ds(piece_from[g * shards + v], size)]
            there = out_ref.at[g, c, pl.ds(piece_to[g * shards + v], size)]

            @pl.when(size > 0)
            def _():
                do(g, here, there)

    v = order[low + step]

    @pl.when(step == 0)
    def _():
        get(step, True)

    @pl.when(step + 1 < steps)
    def _():
        get(step + 1, True)

    for c in range(nc):
        each(v, c, lambda g, here, there: pltpu.make_async_copy(there, here, in_sem.at[c, g]).start())
    onehot = selection(slot_ref[...], slots)
    get(step, False)
    for c in range(nc):
        sorted_rows = jnp.dot(onehot, held[s, c], preferred_element_type=jnp.float32)
        moved[...] = sorted_rows.astype(jnp.bfloat16).reshape(moved.shape)
        each(v, c, lambda g, here, there: pltpu.make_async_copy(there, here, in_sem.at[c, g]).wait())
        old[c] = old[c] + moved[...]
        each(v, c, lambda g, here, there: pltpu.make_async_copy(here, there, out_sem.at[c, g]).start())
    for c in range(nc):
        each(v, c, lambda g, here, there: pltpu.make_async_copy(here, there, out_sem.at[c, g]).wait())


def add_shards(ordered, buffers, places, low, high, plan, first=()):
    source, row, order = places
    nc, _, pairs = buffers[0].shape
    shards, _, shard = plan["slot"].shape
    slots = slots_of(shard)
    return pl.pallas_call(
        functools.partial(add_kernel, len(buffers), low),
        grid_spec=pltpu.PrefetchScalarGridSpec(
            num_scalar_prefetch=6,
            grid=(high - low,),
            in_specs=[
                pl.BlockSpec((1, 1, shard), lambda step, order, *_: (order[low + step], 0, 0))
            ]
            + [pl.BlockSpec(memory_space=pl.ANY)] * (len(buffers) + 1 + len(first)),
            out_specs=pl.BlockSpec(memory_space=pl.ANY),
            scratch_shapes=[
                pltpu.VMEM((2, nc, shard, pairs), jnp.bfloat16),
                pltpu.VMEM((nc, slots // PIECE, PIECE, pairs), jnp.bfloat16),
                pltpu.VMEM((slots // PIECE, PIECE, pairs), jnp.bfloat16),
                pltpu.SemaphoreType.DMA((2, nc)),
                pltpu.SemaphoreType.DMA((nc, LABELS)),
                pltpu.SemaphoreType.DMA((nc, LABELS)),
            ],
        ),
        out_shape=jax.ShapeDtypeStruct(ordered.shape, ordered.dtype),
        input_output_aliases={7 + len(buffers): 0},
        compiler_params=pltpu.CompilerParams(vmem_limit_bytes=VMEM),
        cost_estimate=COST,
        name="add_shards",
    )(
        order, source, row, plan["pieces"].reshape(-1), plan["piece_from"].reshape(-1),
        plan["piece_to"].reshape(-1), plan["slot"], *buffers, ordered, *first,
    )


def multiply_kernel(low, high, span, label, unit, tiles, depth, label_end, label_turn, chunk, origin, *refs):
    count = 4 * (high - low)
    sources, amp_ref = refs[:count], refs[count]
    out_ref, total_ref, held, amp, held_sem, amp_sem = refs[-6:]
    step = pl.program_id(0)
    spare = label.shape[0] - 1
    i = place_of(span, step, spare)
    _, nc, rows, _ = sources[0].shape
    na = rows // RUN
    columns = total_ref.shape[0]
    count, deep = tiles[i], depth[i]
    slot, side = lax.rem(step, 2), lax.rem(label_turn[i], 2)
    follows = label_end[i]

    def get_units(step, start):
        j = place_of(span, step, spare)
        size, s = tiles[j] * depth[j], lax.rem(step, 2)
        for here in range(low, high):

            @pl.when(chunk[j] == here)
            def _():
                for at in range(4):
                    source = sources[4 * (here - low) + at]
                    copy = pltpu.make_async_copy(
                        source.at[pl.ds(unit[j], size)], held.at[s, at, pl.ds(0, size)], held_sem.at[s, at]
                    )
                    copy.start() if start else copy.wait()

    def get_amp(j, start):
        size, s = depth[j] * (TILE // PIECE), lax.rem(label_turn[j], 2)
        for c in range(nc):
            copy = pltpu.make_async_copy(
                amp_ref.at[label[j], c, pl.ds(0, size)], amp.at[s, c, pl.ds(0, size)], amp_sem.at[s, c]
            )
            copy.start() if start else copy.wait()

    active = span[0] + step < span[1]
    opens = active & ((step == 0) | (label[jnp.maximum(i - 1, 0)] != label[i]))

    @pl.when(active & (step == 0))
    def _():
        get_amp(i, True)
        get_units(step, True)

    @pl.when(span[0] + step + 1 < span[1])
    def _():
        get_units(step + 1, True)

    @pl.when(opens & (follows < span[1]))
    def _():
        get_amp(follows, True)

    @pl.when(active)
    def _():
        get_units(step, False)

    @pl.when(opens)
    def _():
        get_amp(i, False)

    def left(c, known):
        parts = []
        for s in range(4):
            for r in range(TILES):
                at = jnp.minimum(r, count - 1) * deep
                parts.append(jnp.concatenate([held[slot, s, at + k, c] for k in range(known)], axis=1))
        return jnp.concatenate(parts, axis=0)

    pieces, _, pairs = amp.shape[2:]
    for known in range(1, pieces * PIECE // TILE + 1):

        @pl.when(active & (deep == known))
        def _():
            lhs = jnp.concatenate([left(c, known) for c in range(nc)], axis=1)
            here = known * TILE // PIECE
            rhs = jnp.concatenate(
                [amp[side, c, :here].reshape(known * TILE, pairs) for c in range(nc)], axis=0
            )
            total = jnp.dot(lhs, rhs, preferred_element_type=jnp.float32)
            for j in range(columns):
                total_ref[j] = total[:, j * TILE : (j + 1) * TILE]

    @pl.when(active)
    def _():
        for s in range(4):
            for a in range(na):
                for j in range(columns):
                    picked = total_ref[j, pl.ds(s * TILES * rows + a, GROUP, stride=na), :]
                    out_ref[(origin[0] ^ s) * na + a, 0, :, j * TILE : (j + 1) * TILE] = (
                        picked.astype(jnp.bfloat16)
                    )


def multiply(sources, amplitudes, plan, origin, low, high, steps, done):
    _, nc, rows, _ = sources[0].shape
    _, _, pieces, piece, pairs = amplitudes.shape
    na = rows // RUN
    window = TILES * pieces * piece // TILE
    most = plan["label"].shape[0]
    spare = most - 1
    out_spec = pl.BlockSpec(
        (4 * na, 1, GROUP, pairs), lambda step, span, *_: (0, place_of(span, step, spare), 0, 0)
    )
    extra = [] if done is None else [done]
    return pl.pallas_call(
        functools.partial(multiply_kernel, low, high),
        grid_spec=pltpu.PrefetchScalarGridSpec(
            num_scalar_prefetch=9,
            grid=(steps,),
            in_specs=[pl.BlockSpec(memory_space=pl.ANY)] * (len(sources) + 1 + len(extra)),
            out_specs=out_spec,
            scratch_shapes=[
                pltpu.VMEM((pairs // TILE, 4 * TILES * rows, TILE), jnp.float32),
                pltpu.VMEM((2, 4, window, nc, rows, TILE), jnp.bfloat16),
                pltpu.VMEM((2, nc, pieces, piece, pairs), jnp.bfloat16),
                pltpu.SemaphoreType.DMA((2, 4)),
                pltpu.SemaphoreType.DMA((2, nc)),
            ],
        ),
        out_shape=jax.ShapeDtypeStruct((4 * na, most, GROUP, pairs), jnp.bfloat16),
        input_output_aliases={10 + len(sources): 0} if extra else {},
        compiler_params=pltpu.CompilerParams(vmem_limit_bytes=VMEM),
        cost_estimate=COST,
        name="multiply",
    )(
        jnp.stack([plan["starts"][low], plan["starts"][high]]), plan["label"], plan["unit"],
        plan["tiles"], plan["depth"], plan["label_end"], plan["label_turn"], plan["chunk"], origin,
        *sources, amplitudes, *extra,
    )


def restore_kernel(live, orbital_ref, in_ref, out_ref, onehot, held):
    slots = orbital_ref.shape[1]
    rows, pairs = out_ref.shape[1:]

    @pl.when(pl.program_id(0) == 0)
    def _():
        place = lax.broadcasted_iota(jnp.int32, (rows, slots), 0)
        onehot[...] = (orbital_ref[...] == place).astype(jnp.float32).astype(jnp.bfloat16)

    sure = rows // GROUP
    for a in range(in_ref.shape[0]):
        for g in range(sure, in_ref.shape[1]):
            kept = jnp.where(g < live[0], in_ref[a, g], jnp.zeros_like(in_ref[a, g]))
            held[a, (g - sure) * GROUP : (g - sure + 1) * GROUP] = kept
        every = jnp.concatenate([in_ref[a, :sure].reshape(rows, pairs), held[a]], axis=0)
        out_ref[a] = jnp.dot(onehot[...], every, preferred_element_type=jnp.float32).astype(jnp.bfloat16)


def restore(grouped, plan, rows):
    block_a, most, _, pairs = grouped.shape
    return pl.pallas_call(
        restore_kernel,
        grid_spec=pltpu.PrefetchScalarGridSpec(
            num_scalar_prefetch=1,
            grid=(block_a // 4,),
            in_specs=[
                pl.BlockSpec((1, most * GROUP), lambda a, *_: (0, 0)),
                pl.BlockSpec((4, most, GROUP, pairs), lambda a, *_: (a, 0, 0, 0)),
            ],
            out_specs=pl.BlockSpec((4, rows, pairs), lambda a, *_: (a, 0, 0)),
            scratch_shapes=[
                pltpu.VMEM((rows, most * GROUP), jnp.bfloat16),
                pltpu.VMEM((4, (most - rows // GROUP) * GROUP, pairs), jnp.bfloat16),
            ],
        ),
        out_shape=jax.ShapeDtypeStruct((block_a, rows, pairs), jnp.bfloat16),
        compiler_params=pltpu.CompilerParams(vmem_limit_bytes=VMEM),
        cost_estimate=COST,
        name="restore",
    )(plan["starts"][-1:], plan["orbital"], grouped)


ORDER = (
    ((-1, 1), (1, 1), (1, 1), (1, 1)),
    ((-1, 2), (-1, 1), (-1, 1), (1, 2)),
    ((-1, 3), (-1, 2), (1, 2), (1, 3)),
)


class Gather:
    def __init__(self, amplitudes, vir, count):
        self.vir, self.count, self.lines = vir, count, count // 2
        self.ups, self.downs, self.across, self.sent = [amplitudes], [amplitudes], [], []

    def step(self, k, tied):
        count, lines, line = self.count, self.lines, self.vir // 2
        new = []
        if k == 0:
            send = self.ups[0]
        else:
            picks = ORDER[k - 1]
            send = self.pick(line, picks)
        if k > 0:
            send = tied(send)
        self.across.append(lax.ppermute(send, "vir", [(i, i ^ 1) for i in range(count)]))
        new.append(self.across[-1])
        if k < lines - 1:
            if k > 0:
                self.ups[k], self.downs[k] = tied(self.ups[k]), tied(self.downs[k])
            up, down = self.ups[k], self.downs[k]
            self.ups.append(lax.ppermute(up, "vir", [(i, i + 2) for i in range(2 * k, count - 2)]))
            self.downs.append(lax.ppermute(down, "vir", [(i, i - 2) for i in range(2, count - 2 * k)]))
            new += [self.ups[-1], self.downs[-1]]
        return new

    def copy(self):
        other = copy.copy(self)
        other.ups, other.downs, other.across = list(self.ups), list(self.downs), list(self.across)
        return other

    def pick(self, line, picks):
        kinds = [self.ups[hop] if way > 0 else self.downs[hop] for way, hop in picks]
        chosen = kinds[0]
        for at in range(1, self.lines):
            if kinds[at] is not kinds[at - 1]:
                chosen = jnp.where(line >= at, kinds[at], chosen)
        return chosen

    def places(self):
        lines, line, count = self.lines, self.vir // 2, self.count
        shards = jnp.arange(count, dtype=jnp.int32)
        ahead = shards // 2 - line
        same = jnp.where(ahead == 0, 0, jnp.where(ahead < 0, -ahead, lines - 1 + ahead))
        turn = jnp.zeros_like(shards)
        for k, picks in enumerate(ORDER):
            for at, (way, hop) in enumerate(picks):
                turn = jnp.where((line == at) & (ahead == -way * hop), k + 1, turn)
        own = shards % 2 == self.vir % 2
        source = jnp.where(own, same, 2 * lines - 1 + turn).astype(jnp.int32)
        step = jnp.where(own, jnp.abs(ahead), turn + 1) * count + shards
        place = jnp.sum((step[:, None] > step[None, :]).astype(jnp.int32), axis=1)
        order = jnp.sum(jnp.where(place[:, None] == shards[None, :], shards[:, None], 0), axis=0)
        return source, jnp.zeros((count,), jnp.int32), order.astype(jnp.int32)

    def buffers(self, k):
        hops = min(k, self.lines - 1)
        blank = [self.ups[0]] * (self.lines - 1 - hops)
        ways = self.ups[: hops + 1] + blank + self.downs[1 : hops + 1] + blank
        return ways + self.across[:k] + [self.ups[0]] * (self.lines - k)


class GatherWhole:
    def __init__(self, amplitudes):
        self.whole = lax.all_gather(amplitudes, "vir", axis=1, tiled=True)

    def copy(self):
        return self

    def step(self, k, tied):
        return []

    def places(self):
        shards = jnp.arange(8, dtype=jnp.int32)
        return jnp.zeros_like(shards), shards * (self.whole.shape[1] // 8), shards

    def buffers(self, k):
        return [self.whole]


def on_device(vir_count, integrals, amplitudes, irrep_labels):
    rows = integrals.shape[1]
    total = irrep_labels.shape[0]
    deepest = -(-(total // 4) // TILE)
    vir, occ = lax.axis_index("vir"), lax.axis_index("occ")
    plan = make_plan(irrep_labels, rows, vir, total // 8, TAILS)
    most = ((rows // RUN + LABELS) * deepest, rows // GROUP + LABELS)
    core = [(i, i ^ 1) for i in range(4)]
    chip = [(i, i ^ 2) for i in range(4)]

    gather = Gather(amplitudes, vir, vir_count) if vir_count == 8 else GatherWhole(amplitudes)
    pairs = -(-deepest // 2)
    sizes = HEAD + (most,)
    last = len(HEAD)
    units, near, far, corner = [], [], [], []
    marks = [None]
    places = gather.places()
    pieces = deepest * TILE // PIECE
    ordered = jnp.zeros(
        (LABELS, amplitudes.shape[0], pieces, PIECE, amplitudes.shape[2]), jnp.bfloat16
    )
    come = (0, 3, 5, 7, 8)

    def tied(array):
        return after(array, marks[-1])

    def packed(at):
        return compact(integrals, plan, at, *sizes[at], pairs, marks[-1:] if at > 1 else [])

    def exchange(at, units):
        return lax.ppermute(units, "occ", chip), lax.ppermute(units, "occ", core)

    units.append(packed(0))
    for k in range(last):
        new = gather.step(k, tied)
        if k > 0:
            units[k] = tied(units[k])
        ahead, beside = exchange(k, units[k])
        far.append(ahead)
        near.append(beside)
        if k > 0:
            far[k - 1] = after(far[k - 1], token(beside, marks[-1]))
            corner.append(lax.ppermute(far[k - 1], "occ", core))
            new.append(corner[-1])
        units.append(packed(k + 1))
        if k > 0:
            ordered = add_shards(
                ordered, gather.buffers(k), places, come[k - 1], come[k], plan, (marks[-1], units[-1])
            )
            new.append(ordered)
        marks.append(token(*new, ahead, beside, units[-1]))

    tail = units.pop()
    origin = occ.astype(jnp.int32).reshape(1)

    def run(size, plan, tail, units, near, far, corner, ordered, before, places):
        far, corner = list(far), list(corner)
        tail = tail[: size[0]]
        mine = gather.copy()
        mine.step(last, lambda array: array)
        ahead, beside = exchange(last, tail)
        far[-1] = after(far[-1], token(beside))
        corner.append(lax.ppermute(far[-1], "occ", core))
        ordered = add_shards(ordered, before, places, come[last - 1], come[last], plan)
        ordered = add_shards(ordered, mine.buffers(last + 1), places, come[last], come[last + 1], plan)
        sources = [one for at in range(last) for one in (units[at], near[at], far[at], corner[at])]
        steps = min(sum(steps for _, steps in HEAD), rows // GROUP + LABELS)
        done = multiply(sources, ordered, plan, origin, 0, last, steps, None)
        ahead = after(ahead, token(done))
        sources = (tail, beside, ahead, lax.ppermute(ahead, "occ", core))
        done = multiply(sources, ordered, plan, origin, last, last + 1, size[1], done)
        return restore(done, plan, rows)

    branches = [functools.partial(run, size) for size in TAILS + (most,)]
    return lax.switch(
        plan["variant"], branches, plan, tail, units, near, far, corner, ordered, gather.buffers(last), places
    )


def solution(mesh):
    in_specs = (P("occ", "vir", None, None), P(None, "vir", "occ"), P())
    out_specs = P(None, "vir", "occ")
    return jax.shard_map(
        functools.partial(on_device, mesh.shape["vir"]),
        mesh=mesh, in_specs=in_specs, out_specs=out_specs, check_vma=False,
    )
```

```python
import functools

import jax
import jax.numpy as jnp
from jax import lax
from jax.experimental import pallas as pl
from jax.experimental.pallas import tpu as pltpu
from jax.sharding import PartitionSpec as P

LABELS = 8
TILE = 128
RUN = 4
TILES = 4
GROUP = RUN * TILES
PIECE = 16
STRIDE = 1024
VMEM = 56 * 2**20
COST = pl.CostEstimate(flops=10**6, bytes_accessed=10**6, transcendentals=0)
CHUNKS = ((56, 6), (128, 12), (128, 12), (152, 18))


def before(values):
    count = values.shape[0]
    earlier = jnp.arange(count)[:, None] > jnp.arange(count)[None, :]
    earlier = earlier.reshape(earlier.shape + (1,) * (values.ndim - 1))
    return jnp.sum(jnp.where(earlier, values[None], 0), axis=1)


def slots_of(shard):
    return -(-(shard + LABELS * 2 * (PIECE - 1)) // TILE) * TILE


def make_plan(labels, rows, vir, shard):
    total = labels.shape[0]
    blocks = total // TILE
    names = jnp.arange(LABELS)
    member = labels.reshape(1, blocks, TILE) == names[:, None, None]
    lower = jnp.arange(TILE)[:, None] < jnp.arange(TILE)[None, :]
    within = jnp.dot(
        member.astype(jnp.bfloat16).reshape(LABELS * blocks, TILE),
        lower.astype(jnp.bfloat16),
        preferred_element_type=jnp.float32,
    )
    within = within.reshape(LABELS, blocks, TILE).astype(jnp.int32)
    held = jnp.sum(member.astype(jnp.int32), axis=2)
    held_before = before(held.T).T
    rank = jnp.sum(jnp.where(member, within + held_before[:, :, None], 0), axis=0).reshape(total)
    sizes = jnp.sum(held, axis=1)
    depth = (sizes + TILE - 1) // TILE

    shards = total // shard
    part = jnp.sum(held.reshape(LABELS, shards, shard // TILE), axis=2)
    part_before = before(part.T).T
    pieces = jnp.where(part > 0, (part_before % PIECE + part + PIECE - 1) // PIECE, 0)
    piece_from = before(pieces)
    piece_to = part_before // PIECE
    move = PIECE * (piece_from - piece_to)
    slot = rank.reshape(shards, shard) + jnp.sum(
        jnp.where(member.reshape(LABELS, shards, shard), move[:, :, None], 0), axis=0
    )

    slices = total // rows
    mine = labels.reshape(1, slices, rows) == names[:, None, None]
    count = jnp.sum(mine.astype(jnp.int32), axis=2)
    row_tiles = (count + RUN - 1) // RUN
    groups = (count + GROUP - 1) // GROUP
    group_from = before(groups)
    unit_from = before(row_tiles * depth[:, None])
    most = rows // GROUP + LABELS + 1
    at = jnp.arange(most)[None, :, None]
    inside = (at >= group_from[:, None]) & (at < (group_from + groups)[:, None])

    def pick(values):
        return jnp.sum(jnp.where(inside, values, 0), axis=0)

    order = jnp.where(inside, at - group_from[:, None], 0)
    group_tiles = pick(jnp.clip(row_tiles[:, None] - TILES * order, 0, TILES))
    group_depth = pick(depth[:, None, None])
    group_unit = pick(unit_from[:, None] + order * TILES * depth[:, None, None])
    group_label = pick(names[:, None, None])
    label_end = pick((group_from + groups)[:, None])
    label_turn = pick(jnp.cumsum((groups > 0).astype(jnp.int32), axis=0)[:, None])
    group_end = group_unit + group_tiles * group_depth
    live = jnp.sum(groups, axis=0)
    valid = jnp.arange(most)[:, None] < live[None]
    starts, bases = [jnp.zeros_like(live)], [jnp.zeros_like(live)]
    for size, steps in CHUNKS:
        fits = valid & (group_end <= (bases[-1] + size)[None])
        fits = fits & (jnp.arange(most)[:, None] < (starts[-1] + steps)[None])
        starts.append(jnp.sum(fits.astype(jnp.int32), axis=0))
        bases.append(jnp.max(jnp.where(fits, group_end, 0), axis=0))
    overflow = jnp.max(live - starts[-1]) > 0
    starts.append(live)
    starts, bases = jnp.stack(starts), jnp.stack(bases)
    chunk = jnp.sum((jnp.arange(most)[:, None, None] >= starts[None, 1:-1]).astype(jnp.int32), axis=1)
    base = jnp.sum(
        jnp.where(chunk[None] == jnp.arange(len(CHUNKS) + 1)[:, None, None], bases[:, None], 0), axis=0
    )

    def own(values):
        return lax.dynamic_index_in_dim(values, vir, axis=values.ndim - 1, keepdims=False)

    group_from, count_before = own(group_from), own(before(count.T).T)
    row_label = lax.dynamic_slice_in_dim(labels, vir * rows, rows, 0)
    row_rank = lax.dynamic_slice_in_dim(rank, vir * rows, rows, 0)
    row_member = row_label[None, :] == names[:, None]
    row_slot = row_rank + jnp.sum(
        jnp.where(row_member, (GROUP * group_from - count_before)[:, None], 0), axis=0
    )
    hit = jnp.arange(most * GROUP)[:, None] == row_slot[None, :]
    orbital = jnp.sum(jnp.where(hit, jnp.arange(rows)[None, :] + 1, 0), axis=1) - 1
    return dict(
        key=(labels * STRIDE + rank).reshape(1, total),
        pieces=pieces.reshape(-1),
        piece_from=piece_from.reshape(-1),
        piece_to=piece_to.reshape(-1),
        slot=slot.reshape(shards, 1, shard),
        label=own(group_label),
        tiles=own(group_tiles),
        depth=own(group_depth),
        unit=own(group_unit - base),
        chunk=own(chunk),
        label_end=own(label_end),
        label_turn=own(label_turn),
        starts=own(starts),
        head=own(jnp.stack([starts[0], starts[-3]])),
        tail=own(jnp.stack([starts[-3], starts[-1]])),
        clamped=jnp.maximum(orbital, 0),
        orbital=orbital.reshape(1, most * GROUP),
        overflow=overflow,
    )


def place_of(span, step, spare):
    return jnp.where(span[1] > span[0], jnp.minimum(span[0] + step, span[1] - 1), spare)


def compact_kernel(span, label, unit, tiles, depth, orbital, key_ref, *refs):
    slabs = refs[:GROUP]
    out_ref, onehot, held, product, stage, sem = refs[-6:]
    step = pl.program_id(0)
    last = pl.num_programs(0) - 1
    i = place_of(span, step, label.shape[0] - 1)
    na, _, nc, width = slabs[0].shape
    rows = na * nc
    slot = lax.rem(step, 2)
    deep, name = depth[i], label[i]

    def active(step):
        return span[0] + step < span[1]

    @pl.when(active(step) & ((step == 0) | (label[jnp.maximum(i - 1, 0)] != name)))
    def _():
        def build(k, carry):
            place = lax.broadcasted_iota(jnp.int32, (2 * TILE, width), 0)
            place = place + (name * STRIDE + k * 2 * TILE)
            onehot[k] = (key_ref[...] == place).astype(jnp.float32).astype(jnp.bfloat16)
            return carry

        lax.fori_loop(0, (deep + 1) // 2, build, 0)

    def copy(step, s):
        j = place_of(span, step, label.shape[0] - 1)
        size = tiles[j] * depth[j]
        return pltpu.make_async_copy(
            stage.at[s, pl.ds(0, size)], out_ref.at[pl.ds(unit[j], size)], sem.at[s]
        )

    @pl.when((step >= 2) & active(step - 2))
    def _():
        copy(step - 2, slot).wait()

    @pl.when(active(step))
    def _():
        for r in range(GROUP):
            held[r * rows : (r + 1) * rows, :] = slabs[r][...].reshape(rows, width)

        def part(k, carry):
            full = lax.dot_general(
                held[...], onehot[k], (((1,), (1,)), ((), ())), preferred_element_type=jnp.float32
            )
            for h in range(2):
                product[h] = full[:, h * TILE : (h + 1) * TILE]
            for h in range(2):

                @pl.when(2 * k + h < deep)
                def _():
                    for c in range(nc):
                        one = product[h, pl.ds(c, GROUP * na, stride=nc), :].astype(jnp.bfloat16)
                        for r in range(TILES):
                            stage[slot, r * deep + 2 * k + h, c] = one[
                                r * RUN * na : (r + 1) * RUN * na
                            ]

            return carry

        lax.fori_loop(0, (deep + 1) // 2, part, 0)
        copy(step, slot).start()

    @pl.when((step == last) & (step >= 1) & active(step - 1))
    def _():
        copy(step - 1, 1 - slot).wait()

    @pl.when((step == last) & active(step))
    def _():
        copy(step, slot).wait()


def token(*arrays):
    def kernel(*refs):
        refs[-1][...] = jnp.zeros_like(refs[-1])

    return pl.pallas_call(
        kernel,
        in_specs=[pl.BlockSpec(memory_space=pl.ANY)] * len(arrays),
        out_shape=jax.ShapeDtypeStruct((8, TILE), jnp.float32),
        cost_estimate=COST,
        name="token",
    )(*arrays)


def unset(shape, *marks):
    def kernel(*refs):
        del refs

    return pl.pallas_call(
        kernel,
        in_specs=[pl.BlockSpec(memory_space=pl.ANY)] * len(marks),
        out_specs=pl.BlockSpec(memory_space=pl.ANY),
        out_shape=jax.ShapeDtypeStruct(shape, jnp.bfloat16),
        cost_estimate=COST,
        name="unset",
    )(*marks)


def after(array, mark):
    def kernel(*refs):
        del refs

    return pl.pallas_call(
        kernel,
        in_specs=[pl.BlockSpec(memory_space=pl.ANY)] * 2,
        out_specs=pl.BlockSpec(memory_space=pl.ANY),
        out_shape=jax.ShapeDtypeStruct(array.shape, array.dtype),
        input_output_aliases={0: 0},
        cost_estimate=COST,
        name="after",
    )(array, mark)


def compact(integrals, plan, span, size, steps, pairs, first):
    na, rows, nc, width = integrals.shape
    spare = plan["label"].shape[0] - 1

    def slab(r):
        def at(step, span, label, unit, tiles, depth, orbital):
            return 0, orbital[place_of(span, step, spare) * GROUP + r], 0, 0

        return pl.BlockSpec((na, 1, nc, width), at)

    return pl.pallas_call(
        compact_kernel,
        grid_spec=pltpu.PrefetchScalarGridSpec(
            num_scalar_prefetch=6,
            grid=(steps,),
            in_specs=[pl.BlockSpec((1, width), lambda step, *_: (0, 0))]
            + [slab(r) for r in range(GROUP)]
            + [pl.BlockSpec(memory_space=pl.ANY)] * len(first),
            out_specs=pl.BlockSpec(memory_space=pl.ANY),
            scratch_shapes=[
                pltpu.VMEM((pairs, 2 * TILE, width), jnp.bfloat16),
                pltpu.VMEM((GROUP * na * nc, width), jnp.bfloat16),
                pltpu.VMEM((2, GROUP * na * nc, TILE), jnp.float32),
                pltpu.VMEM((2, TILES * 2 * pairs, nc, RUN * na, TILE), jnp.bfloat16),
                pltpu.SemaphoreType.DMA((2,)),
            ],
        ),
        out_shape=jax.ShapeDtypeStruct((size, nc, RUN * na, TILE), jnp.bfloat16),
        compiler_params=pltpu.CompilerParams(vmem_limit_bytes=VMEM),
        cost_estimate=COST,
        name="compact",
    )(
        span, plan["label"], plan["unit"], plan["tiles"], plan["depth"], plan["clamped"], plan["key"], *([integrals] * GROUP), *first,
    )


def fetch(buffers, source, row, v, c, held, sem, start):
    width = held.shape[0]
    for at in range(len(buffers)):

        @pl.when(source[v] == at)
        def _():
            rows = pl.ds(pl.multiple_of(row[v], width), width)
            copy = pltpu.make_async_copy(buffers[at].at[c, rows], held, sem)
            if start:
                copy.start()
            else:
                copy.wait()


def selection(slot, slots):
    width = slot.shape[-1]
    place = lax.broadcasted_iota(jnp.int32, (slots, width), 0)
    return (slot.reshape(1, width) == place).astype(jnp.float32).astype(jnp.bfloat16)


def add_kernel(nbuf, low, order, source, row, pieces, piece_from, piece_to, slot_ref, *refs):
    buffers = refs[:nbuf]
    out_ref, held, old, moved, sem, in_sem, out_sem = refs[-7:]
    shards = order.shape[0]
    step = pl.program_id(0)
    steps = pl.num_programs(0)
    nc = old.shape[0]
    slots = old.shape[1] * PIECE
    s = lax.rem(step, 2)

    def get(step, start):
        for c in range(nc):
            h = lax.rem(step, 2)
            fetch(buffers, source, row, order[low + step], c, held.at[h, c], sem.at[h, c], start)

    def each(v, c, do):
        for g in range(LABELS):
            size = pieces[g * shards + v]
            here = old.at[c, pl.ds(piece_from[g * shards + v], size)]
            there = out_ref.at[g, c, pl.ds(piece_to[g * shards + v], size)]

            @pl.when(size > 0)
            def _():
                do(g, here, there)

    v = order[low + step]

    @pl.when(step == 0)
    def _():
        get(step, True)

    @pl.when(step + 1 < steps)
    def _():
        get(step + 1, True)

    for c in range(nc):
        each(v, c, lambda g, here, there: pltpu.make_async_copy(there, here, in_sem.at[c, g]).start())
    onehot = selection(slot_ref[...], slots)
    get(step, False)
    for c in range(nc):
        sorted_rows = jnp.dot(onehot, held[s, c], preferred_element_type=jnp.float32)
        moved[...] = sorted_rows.astype(jnp.bfloat16).reshape(moved.shape)
        each(v, c, lambda g, here, there: pltpu.make_async_copy(there, here, in_sem.at[c, g]).wait())
        old[c] = old[c] + moved[...]
        each(v, c, lambda g, here, there: pltpu.make_async_copy(here, there, out_sem.at[c, g]).start())
    for c in range(nc):
        each(v, c, lambda g, here, there: pltpu.make_async_copy(here, there, out_sem.at[c, g]).wait())


def add_shards(ordered, buffers, places, low, high, plan, first=()):
    source, row, order = places
    nc, _, pairs = buffers[0].shape
    shards, _, shard = plan["slot"].shape
    slots = slots_of(shard)
    return pl.pallas_call(
        functools.partial(add_kernel, len(buffers), low),
        grid_spec=pltpu.PrefetchScalarGridSpec(
            num_scalar_prefetch=6,
            grid=(high - low,),
            in_specs=[
                pl.BlockSpec((1, 1, shard), lambda step, order, *_: (order[low + step], 0, 0))
            ]
            + [pl.BlockSpec(memory_space=pl.ANY)] * (len(buffers) + 1 + len(first)),
            out_specs=pl.BlockSpec(memory_space=pl.ANY),
            scratch_shapes=[
                pltpu.VMEM((2, nc, shard, pairs), jnp.bfloat16),
                pltpu.VMEM((nc, slots // PIECE, PIECE, pairs), jnp.bfloat16),
                pltpu.VMEM((slots // PIECE, PIECE, pairs), jnp.bfloat16),
                pltpu.SemaphoreType.DMA((2, nc)),
                pltpu.SemaphoreType.DMA((nc, LABELS)),
                pltpu.SemaphoreType.DMA((nc, LABELS)),
            ],
        ),
        out_shape=jax.ShapeDtypeStruct(ordered.shape, ordered.dtype),
        input_output_aliases={7 + len(buffers): 0},
        compiler_params=pltpu.CompilerParams(vmem_limit_bytes=VMEM),
        cost_estimate=COST,
        name="add_shards",
    )(
        order, source, row, plan["pieces"], plan["piece_from"], plan["piece_to"], plan["slot"], *buffers, ordered, *first,
    )


def multiply_kernel(low, high, span, label, unit, tiles, depth, label_end, label_turn, chunk, origin, *refs):
    count = 4 * (high - low)
    sources, amp_ref = refs[:count], refs[count]
    out_ref, total_ref, held, amp, held_sem, amp_sem = refs[-6:]
    step = pl.program_id(0)
    spare = label.shape[0] - 1
    i = place_of(span, step, spare)
    _, nc, rows, _ = sources[0].shape
    na = rows // RUN
    columns = total_ref.shape[0]
    count, deep = tiles[i], depth[i]
    slot, side = lax.rem(step, 2), lax.rem(label_turn[i], 2)
    follows = label_end[i]

    def get_units(step, start):
        j = place_of(span, step, spare)
        size, s = tiles[j] * depth[j], lax.rem(step, 2)
        for here in range(low, high):

            @pl.when(chunk[j] == here)
            def _():
                for at in range(4):
                    source = sources[4 * (here - low) + at]
                    copy = pltpu.make_async_copy(
                        source.at[pl.ds(unit[j], size)], held.at[s, at, pl.ds(0, size)], held_sem.at[s, at]
                    )
                    copy.start() if start else copy.wait()

    def get_amp(j, start):
        size, s = depth[j] * (TILE // PIECE), lax.rem(label_turn[j], 2)
        for c in range(nc):
            copy = pltpu.make_async_copy(
                amp_ref.at[label[j], c, pl.ds(0, size)], amp.at[s, c, pl.ds(0, size)], amp_sem.at[s, c]
            )
            copy.start() if start else copy.wait()

    active = span[0] + step < span[1]
    opens = active & ((step == 0) | (label[jnp.maximum(i - 1, 0)] != label[i]))

    @pl.when(active & (step == 0))
    def _():
        get_amp(i, True)
        get_units(step, True)

    @pl.when(span[0] + step + 1 < span[1])
    def _():
        get_units(step + 1, True)

    @pl.when(opens & (follows < span[1]))
    def _():
        get_amp(follows, True)

    @pl.when(active)
    def _():
        get_units(step, False)

    @pl.when(opens)
    def _():
        get_amp(i, False)

    def left(c, known):
        parts = []
        for s in range(4):
            for r in range(TILES):
                at = jnp.minimum(r, count - 1) * deep
                parts.append(jnp.concatenate([held[slot, s, at + k, c] for k in range(known)], axis=1))
        return jnp.concatenate(parts, axis=0)

    pieces, _, pairs = amp.shape[2:]
    for known in range(1, pieces * PIECE // TILE + 1):

        @pl.when(active & (deep == known))
        def _():
            lhs = jnp.concatenate([left(c, known) for c in range(nc)], axis=1)
            here = known * TILE // PIECE
            rhs = jnp.concatenate(
                [amp[side, c, :here].reshape(known * TILE, pairs) for c in range(nc)], axis=0
            )
            total = jnp.dot(lhs, rhs, preferred_element_type=jnp.float32)
            for j in range(columns):
                total_ref[j] = total[:, j * TILE : (j + 1) * TILE]

    @pl.when(active)
    def _():
        for s in range(4):
            for a in range(na):
                for j in range(columns):
                    picked = total_ref[j, pl.ds(s * TILES * rows + a, GROUP, stride=na), :]
                    out_ref[(origin[0] ^ s) * na + a, 0, :, j * TILE : (j + 1) * TILE] = (
                        picked.astype(jnp.bfloat16)
                    )


def multiply(sources, amplitudes, plan, origin, span, low, high, steps, done):
    _, nc, rows, _ = sources[0].shape
    _, _, pieces, piece, pairs = amplitudes.shape
    na = rows // RUN
    window = TILES * pieces * piece // TILE
    most = plan["label"].shape[0]
    spare = most - 1
    out_spec = pl.BlockSpec(
        (4 * na, 1, GROUP, pairs), lambda step, span, *_: (0, place_of(span, step, spare), 0, 0)
    )
    extra = [] if done is None else [done]
    return pl.pallas_call(
        functools.partial(multiply_kernel, low, high),
        grid_spec=pltpu.PrefetchScalarGridSpec(
            num_scalar_prefetch=9,
            grid=(steps,),
            in_specs=[pl.BlockSpec(memory_space=pl.ANY)] * (len(sources) + 1 + len(extra)),
            out_specs=out_spec,
            scratch_shapes=[
                pltpu.VMEM((pairs // TILE, 4 * TILES * rows, TILE), jnp.float32),
                pltpu.VMEM((2, 4, window, nc, rows, TILE), jnp.bfloat16),
                pltpu.VMEM((2, nc, pieces, piece, pairs), jnp.bfloat16),
                pltpu.SemaphoreType.DMA((2, 4)),
                pltpu.SemaphoreType.DMA((2, nc)),
            ],
        ),
        out_shape=jax.ShapeDtypeStruct((4 * na, most, GROUP, pairs), jnp.bfloat16),
        input_output_aliases={10 + len(sources): 0} if extra else {},
        compiler_params=pltpu.CompilerParams(vmem_limit_bytes=VMEM),
        cost_estimate=COST,
        name="multiply",
    )(
        span, plan["label"], plan["unit"],
        plan["tiles"], plan["depth"], plan["label_end"], plan["label_turn"], plan["chunk"], origin,
        *sources, amplitudes, *extra,
    )


def restore_kernel(live, orbital_ref, in_ref, out_ref, onehot, held):
    slots = orbital_ref.shape[1]
    rows, pairs = out_ref.shape[1:]

    @pl.when(pl.program_id(0) == 0)
    def _():
        place = lax.broadcasted_iota(jnp.int32, (rows, slots), 0)
        onehot[...] = (orbital_ref[...] == place).astype(jnp.float32).astype(jnp.bfloat16)

    sure = rows // GROUP
    for a in range(in_ref.shape[0]):
        for g in range(sure, in_ref.shape[1]):
            kept = jnp.where(g < live[0], in_ref[a, g], jnp.zeros_like(in_ref[a, g]))
            held[a, (g - sure) * GROUP : (g - sure + 1) * GROUP] = kept
        every = jnp.concatenate([in_ref[a, :sure].reshape(rows, pairs), held[a]], axis=0)
        out_ref[a] = jnp.dot(onehot[...], every, preferred_element_type=jnp.float32).astype(jnp.bfloat16)


def restore(grouped, plan, rows):
    block_a, most, _, pairs = grouped.shape
    return pl.pallas_call(
        restore_kernel,
        grid_spec=pltpu.PrefetchScalarGridSpec(
            num_scalar_prefetch=1,
            grid=(block_a // 4,),
            in_specs=[
                pl.BlockSpec((1, most * GROUP), lambda a, *_: (0, 0)),
                pl.BlockSpec((4, most, GROUP, pairs), lambda a, *_: (a, 0, 0, 0)),
            ],
            out_specs=pl.BlockSpec((4, rows, pairs), lambda a, *_: (a, 0, 0)),
            scratch_shapes=[
                pltpu.VMEM((rows, most * GROUP), jnp.bfloat16),
                pltpu.VMEM((4, (most - rows // GROUP) * GROUP, pairs), jnp.bfloat16),
            ],
        ),
        out_shape=jax.ShapeDtypeStruct((block_a, rows, pairs), jnp.bfloat16),
        compiler_params=pltpu.CompilerParams(vmem_limit_bytes=VMEM),
        cost_estimate=COST,
        name="restore",
    )(plan["starts"][-1:], plan["orbital"], grouped)


ORDER = (
    ((-1, 1), (1, 1), (1, 1), (1, 1)),
    ((-1, 2), (-1, 1), (-1, 1), (1, 2)),
    ((-1, 3), (-1, 2), (1, 2), (1, 3)),
)


class Gather:
    def __init__(self, amplitudes, vir, count):
        self.vir, self.count, self.lines = vir, count, count // 2
        self.ups, self.downs, self.across, self.sent = [amplitudes], [amplitudes], [], []

    def step(self, k, tied):
        count, lines, line = self.count, self.lines, self.vir // 2
        new = []
        if k == 0:
            send = self.ups[0]
        else:
            picks = ORDER[k - 1]
            send = self.pick(line, picks)
        if k > 0:
            send = tied(send)
        self.across.append(lax.ppermute(send, "vir", [(i, i ^ 1) for i in range(count)]))
        new.append(self.across[-1])
        if k < lines - 1:
            if k > 0:
                self.ups[k], self.downs[k] = tied(self.ups[k]), tied(self.downs[k])
            up, down = self.ups[k], self.downs[k]
            self.ups.append(lax.ppermute(up, "vir", [(i, i + 2) for i in range(2 * k, count - 2)]))
            self.downs.append(lax.ppermute(down, "vir", [(i, i - 2) for i in range(2, count - 2 * k)]))
            new += [self.ups[-1], self.downs[-1]]
        return new

    def pick(self, line, picks):
        kinds = [self.ups[hop] if way > 0 else self.downs[hop] for way, hop in picks]
        chosen = kinds[0]
        for at in range(1, self.lines):
            if kinds[at] is not kinds[at - 1]:
                chosen = jnp.where(line >= at, kinds[at], chosen)
        return chosen

    def places(self):
        lines, line, count = self.lines, self.vir // 2, self.count
        shards = jnp.arange(count, dtype=jnp.int32)
        ahead = shards // 2 - line
        same = jnp.where(ahead == 0, 0, jnp.where(ahead < 0, -ahead, lines - 1 + ahead))
        turn = jnp.zeros_like(shards)
        for k, picks in enumerate(ORDER):
            for at, (way, hop) in enumerate(picks):
                turn = jnp.where((line == at) & (ahead == -way * hop), k + 1, turn)
        own = shards % 2 == self.vir % 2
        source = jnp.where(own, same, 2 * lines - 1 + turn).astype(jnp.int32)
        step = jnp.where(own, jnp.abs(ahead), turn + 1) * count + shards
        place = jnp.sum((step[:, None] > step[None, :]).astype(jnp.int32), axis=1)
        order = jnp.sum(jnp.where(place[:, None] == shards[None, :], shards[:, None], 0), axis=0)
        return source, jnp.zeros((count,), jnp.int32), order.astype(jnp.int32)

    def buffers(self, k):
        hops = min(k, self.lines - 1)
        blank = [self.ups[0]] * (self.lines - 1 - hops)
        ways = self.ups[: hops + 1] + blank + self.downs[1 : hops + 1] + blank
        return ways + self.across[:k] + [self.ups[0]] * (self.lines - k)


class GatherWhole:
    def __init__(self, amplitudes):
        self.whole = lax.all_gather(amplitudes, "vir", axis=1, tiled=True)

    def step(self, k, tied):
        return []

    def places(self):
        shards = jnp.arange(8, dtype=jnp.int32)
        return jnp.zeros_like(shards), shards * (self.whole.shape[1] // 8), shards

    def buffers(self, k):
        return [self.whole]


def on_device(vir_count, integrals, amplitudes, irrep_labels):
    rows = integrals.shape[1]
    total = irrep_labels.shape[0]
    deepest = -(-(total // 4) // TILE)
    vir, occ = lax.axis_index("vir"), lax.axis_index("occ")
    plan = make_plan(irrep_labels, rows, vir, total // 8)
    most = ((rows // RUN + LABELS) * deepest, rows // GROUP + LABELS)
    core = [(i, i ^ 1) for i in range(4)]
    chip = [(i, i ^ 2) for i in range(4)]

    gather = Gather(amplitudes, vir, vir_count) if vir_count == 8 else GatherWhole(amplitudes)
    pairs = -(-deepest // 2)
    last = len(CHUNKS) - 1
    units, near, far, corner = [], [], [], []
    marks = [None]
    places = gather.places()
    pieces = deepest * TILE // PIECE
    ordered = jnp.zeros(
        (LABELS, amplitudes.shape[0], pieces, PIECE, amplitudes.shape[2]), jnp.bfloat16
    )
    come = (0, 1, 2, 7, 8)

    def tied(array):
        return after(array, marks[-1])

    def packed(at):
        span = plan["starts"][at : at + 2]
        return compact(integrals, plan, span, *CHUNKS[at], pairs, marks[-1:] if at > 1 else [])

    def exchange(at, units):
        return lax.ppermute(units, "occ", chip), lax.ppermute(units, "occ", core)

    units.append(packed(0))
    for k in range(last):
        new = gather.step(k, tied)
        if k > 0:
            units[k] = tied(units[k])
        ahead, beside = exchange(k, units[k])
        far.append(ahead)
        near.append(beside)
        if k > 0:
            far[k - 1] = after(far[k - 1], token(beside, marks[-1]))
            corner.append(lax.ppermute(far[k - 1], "occ", core))
            new.append(corner[-1])
        units.append(packed(k + 1))
        if k > 0:
            ordered = add_shards(
                ordered, gather.buffers(k), places, come[k - 1], come[k], plan, (marks[-1], units[-1])
            )
            new.append(ordered)
        marks.append(token(*new, ahead, beside, units[-1]))

    origin = occ.astype(jnp.int32).reshape(1)
    before = gather.buffers(last)
    gather.step(last, tied)
    ahead, beside = exchange(last, units[last])
    far.append(ahead)
    near.append(beside)
    corner.append(lax.ppermute(far[last - 1], "occ", core))
    ordered = add_shards(ordered, before, places, come[last - 1], come[last], plan)

    def more(*buffers):
        own = compact(integrals, plan, plan["starts"][last + 1 :], *most, pairs, [])
        ahead, beside = exchange(last + 1, own)
        return own, beside, ahead, lax.ppermute(ahead, "occ", core)

    shape = (most[0], *units[0].shape[1:])
    extra = unset(shape, token(ordered)), unset(shape), unset(shape), unset(shape)
    extra = lax.cond(plan["overflow"], more, lambda *buffers: buffers, *extra)
    ordered = add_shards(ordered, gather.buffers(last + 1), places, come[last], come[last + 1], plan)
    sources = [one for at in range(last) for one in (units[at], near[at], far[at], corner[at])]
    steps = min(sum(steps for _, steps in CHUNKS[:last]), rows // GROUP + LABELS)
    done = multiply(sources, ordered, plan, origin, plan["head"], 0, last, steps, None)
    far[last] = after(far[last], token(done))
    corner.append(lax.ppermute(far[last], "occ", core))
    sources = (units[last], near[last], far[last], corner[last], *extra)
    done = multiply(sources, ordered, plan, origin, plan["tail"], last, last + 2, most[1], done)
    return restore(done, plan, rows)


def solution(mesh):
    in_specs = (P("occ", "vir", None, None), P(None, "vir", "occ"), P())
    out_specs = P(None, "vir", "occ")
    return jax.shard_map(
        functools.partial(on_device, mesh.shape["vir"]),
        mesh=mesh, in_specs=in_specs, out_specs=out_specs, check_vma=False,
    )
```

```python
import functools

import jax
import jax.numpy as jnp
from jax import lax
from jax.experimental import pallas as pl
from jax.experimental.pallas import tpu as pltpu
from jax.sharding import PartitionSpec as P

LABELS = 8
TILE = 128
RUN = 4
TILES = 4
GROUP = RUN * TILES
PIECE = 16
STRIDE = 1024
VMEM = 56 * 2**20
COST = pl.CostEstimate(flops=10**6, bytes_accessed=10**6, transcendentals=0)
CHUNKS = ((48, 5), (104, 10), (104, 10), (192, 20))


def before(values):
    count = values.shape[0]
    earlier = jnp.arange(count)[:, None] > jnp.arange(count)[None, :]
    earlier = earlier.reshape(earlier.shape + (1,) * (values.ndim - 1))
    return jnp.sum(jnp.where(earlier, values[None], 0), axis=1)


def slots_of(shard):
    return -(-(shard + LABELS * 2 * (PIECE - 1)) // TILE) * TILE


def make_plan(labels, rows, vir, shard):
    total = labels.shape[0]
    blocks = total // TILE
    names = jnp.arange(LABELS)
    member = labels.reshape(1, blocks, TILE) == names[:, None, None]
    lower = jnp.arange(TILE)[:, None] < jnp.arange(TILE)[None, :]
    within = jnp.dot(
        member.astype(jnp.bfloat16).reshape(LABELS * blocks, TILE),
        lower.astype(jnp.bfloat16),
        preferred_element_type=jnp.float32,
    )
    within = within.reshape(LABELS, blocks, TILE).astype(jnp.int32)
    held = jnp.sum(member.astype(jnp.int32), axis=2)
    held_before = before(held.T).T
    rank = jnp.sum(jnp.where(member, within + held_before[:, :, None], 0), axis=0).reshape(total)
    sizes = jnp.sum(held, axis=1)
    depth = (sizes + TILE - 1) // TILE

    shards = total // shard
    part = jnp.sum(held.reshape(LABELS, shards, shard // TILE), axis=2)
    part_before = before(part.T).T
    pieces = jnp.where(part > 0, (part_before % PIECE + part + PIECE - 1) // PIECE, 0)
    piece_from = before(pieces)
    piece_to = part_before // PIECE
    move = PIECE * (piece_from - piece_to)
    slot = rank.reshape(shards, shard) + jnp.sum(
        jnp.where(member.reshape(LABELS, shards, shard), move[:, :, None], 0), axis=0
    )

    slices = total // rows
    mine = labels.reshape(1, slices, rows) == names[:, None, None]
    count = jnp.sum(mine.astype(jnp.int32), axis=2)
    row_tiles = (count + RUN - 1) // RUN
    groups = (count + GROUP - 1) // GROUP
    group_from = before(groups)
    unit_from = before(row_tiles * depth[:, None])
    most = rows // GROUP + LABELS + 1
    at = jnp.arange(most)[None, :, None]
    inside = (at >= group_from[:, None]) & (at < (group_from + groups)[:, None])

    def pick(values):
        return jnp.sum(jnp.where(inside, values, 0), axis=0)

    order = jnp.where(inside, at - group_from[:, None], 0)
    group_tiles = pick(jnp.clip(row_tiles[:, None] - TILES * order, 0, TILES))
    group_depth = pick(depth[:, None, None])
    group_unit = pick(unit_from[:, None] + order * TILES * depth[:, None, None])
    group_label = pick(names[:, None, None])
    label_end = pick((group_from + groups)[:, None])
    label_turn = pick(jnp.cumsum((groups > 0).astype(jnp.int32), axis=0)[:, None])
    group_end = group_unit + group_tiles * group_depth
    live = jnp.sum(groups, axis=0)
    valid = jnp.arange(most)[:, None] < live[None]
    starts, bases = [jnp.zeros_like(live)], [jnp.zeros_like(live)]
    for size, steps in CHUNKS:
        fits = valid & (group_end <= (bases[-1] + size)[None])
        fits = fits & (jnp.arange(most)[:, None] < (starts[-1] + steps)[None])
        starts.append(jnp.sum(fits.astype(jnp.int32), axis=0))
        bases.append(jnp.max(jnp.where(fits, group_end, 0), axis=0))
    overflow = jnp.max(live - starts[-1]) > 0
    starts.append(live)
    starts, bases = jnp.stack(starts), jnp.stack(bases)
    chunk = jnp.sum((jnp.arange(most)[:, None, None] >= starts[None, 1:-1]).astype(jnp.int32), axis=1)
    base = jnp.sum(
        jnp.where(chunk[None] == jnp.arange(len(CHUNKS) + 1)[:, None, None], bases[:, None], 0), axis=0
    )

    def own(values):
        return lax.dynamic_index_in_dim(values, vir, axis=values.ndim - 1, keepdims=False)

    group_from, count_before = own(group_from), own(before(count.T).T)
    row_label = lax.dynamic_slice_in_dim(labels, vir * rows, rows, 0)
    row_rank = lax.dynamic_slice_in_dim(rank, vir * rows, rows, 0)
    row_member = row_label[None, :] == names[:, None]
    row_slot = row_rank + jnp.sum(
        jnp.where(row_member, (GROUP * group_from - count_before)[:, None], 0), axis=0
    )
    hit = jnp.arange(most * GROUP)[:, None] == row_slot[None, :]
    orbital = jnp.sum(jnp.where(hit, jnp.arange(rows)[None, :] + 1, 0), axis=1) - 1
    return dict(
        key=(labels * STRIDE + rank).reshape(1, total),
        pieces=pieces.reshape(-1),
        piece_from=piece_from.reshape(-1),
        piece_to=piece_to.reshape(-1),
        slot=slot.reshape(shards, 1, shard),
        label=own(group_label),
        tiles=own(group_tiles),
        depth=own(group_depth),
        unit=own(group_unit - base),
        chunk=own(chunk),
        label_end=own(label_end),
        label_turn=own(label_turn),
        starts=own(starts),
        head=own(jnp.stack([starts[0], starts[-3]])),
        tail=own(jnp.stack([starts[-3], starts[-1]])),
        clamped=jnp.maximum(orbital, 0),
        orbital=orbital.reshape(1, most * GROUP),
        overflow=overflow,
    )


def place_of(span, step, spare):
    return jnp.where(span[1] > span[0], jnp.minimum(span[0] + step, span[1] - 1), spare)


def compact_kernel(span, label, unit, tiles, depth, orbital, key_ref, *refs):
    slabs = refs[:GROUP]
    out_ref, onehot, held, product, stage, sem = refs[-6:]
    step = pl.program_id(0)
    last = pl.num_programs(0) - 1
    i = place_of(span, step, label.shape[0] - 1)
    na, _, nc, width = slabs[0].shape
    rows = na * nc
    slot = lax.rem(step, 2)
    deep, name = depth[i], label[i]

    def active(step):
        return span[0] + step < span[1]

    @pl.when(active(step) & ((step == 0) | (label[jnp.maximum(i - 1, 0)] != name)))
    def _():
        def build(k, carry):
            place = lax.broadcasted_iota(jnp.int32, (2 * TILE, width), 0)
            place = place + (name * STRIDE + k * 2 * TILE)
            onehot[k] = (key_ref[...] == place).astype(jnp.float32).astype(jnp.bfloat16)
            return carry

        lax.fori_loop(0, (deep + 1) // 2, build, 0)

    def copy(step, s):
        j = place_of(span, step, label.shape[0] - 1)
        size = tiles[j] * depth[j]
        return pltpu.make_async_copy(
            stage.at[s, pl.ds(0, size)], out_ref.at[pl.ds(unit[j], size)], sem.at[s]
        )

    @pl.when((step >= 2) & active(step - 2))
    def _():
        copy(step - 2, slot).wait()

    @pl.when(active(step))
    def _():
        for r in range(GROUP):
            held[r * rows : (r + 1) * rows, :] = slabs[r][...].reshape(rows, width)

        def part(k, carry):
            full = lax.dot_general(
                held[...], onehot[k], (((1,), (1,)), ((), ())), preferred_element_type=jnp.float32
            )
            for h in range(2):
                product[h] = full[:, h * TILE : (h + 1) * TILE]
            for h in range(2):

                @pl.when(2 * k + h < deep)
                def _():
                    for c in range(nc):
                        one = product[h, pl.ds(c, GROUP * na, stride=nc), :].astype(jnp.bfloat16)
                        for r in range(TILES):
                            stage[slot, r * deep + 2 * k + h, c] = one[
                                r * RUN * na : (r + 1) * RUN * na
                            ]

            return carry

        lax.fori_loop(0, (deep + 1) // 2, part, 0)
        copy(step, slot).start()

    @pl.when((step == last) & (step >= 1) & active(step - 1))
    def _():
        copy(step - 1, 1 - slot).wait()

    @pl.when((step == last) & active(step))
    def _():
        copy(step, slot).wait()


def token(*arrays):
    def kernel(*refs):
        refs[-1][...] = jnp.zeros_like(refs[-1])

    return pl.pallas_call(
        kernel,
        in_specs=[pl.BlockSpec(memory_space=pl.ANY)] * len(arrays),
        out_shape=jax.ShapeDtypeStruct((8, TILE), jnp.float32),
        cost_estimate=COST,
        name="token",
    )(*arrays)


def unset(shape, *marks):
    def kernel(*refs):
        del refs

    return pl.pallas_call(
        kernel,
        in_specs=[pl.BlockSpec(memory_space=pl.ANY)] * len(marks),
        out_specs=pl.BlockSpec(memory_space=pl.ANY),
        out_shape=jax.ShapeDtypeStruct(shape, jnp.bfloat16),
        cost_estimate=COST,
        name="unset",
    )(*marks)


def after(array, mark):
    def kernel(*refs):
        del refs

    return pl.pallas_call(
        kernel,
        in_specs=[pl.BlockSpec(memory_space=pl.ANY)] * 2,
        out_specs=pl.BlockSpec(memory_space=pl.ANY),
        out_shape=jax.ShapeDtypeStruct(array.shape, array.dtype),
        input_output_aliases={0: 0},
        cost_estimate=COST,
        name="after",
    )(array, mark)


def compact(integrals, plan, span, size, steps, pairs, first):
    na, rows, nc, width = integrals.shape
    spare = plan["label"].shape[0] - 1

    def slab(r):
        def at(step, span, label, unit, tiles, depth, orbital):
            return 0, orbital[place_of(span, step, spare) * GROUP + r], 0, 0

        return pl.BlockSpec((na, 1, nc, width), at)

    return pl.pallas_call(
        compact_kernel,
        grid_spec=pltpu.PrefetchScalarGridSpec(
            num_scalar_prefetch=6,
            grid=(steps,),
            in_specs=[pl.BlockSpec((1, width), lambda step, *_: (0, 0))]
            + [slab(r) for r in range(GROUP)]
            + [pl.BlockSpec(memory_space=pl.ANY)] * len(first),
            out_specs=pl.BlockSpec(memory_space=pl.ANY),
            scratch_shapes=[
                pltpu.VMEM((pairs, 2 * TILE, width), jnp.bfloat16),
                pltpu.VMEM((GROUP * na * nc, width), jnp.bfloat16),
                pltpu.VMEM((2, GROUP * na * nc, TILE), jnp.float32),
                pltpu.VMEM((2, TILES * 2 * pairs, nc, RUN * na, TILE), jnp.bfloat16),
                pltpu.SemaphoreType.DMA((2,)),
            ],
        ),
        out_shape=jax.ShapeDtypeStruct((size, nc, RUN * na, TILE), jnp.bfloat16),
        compiler_params=pltpu.CompilerParams(vmem_limit_bytes=VMEM),
        cost_estimate=COST,
        name="compact",
    )(
        span, plan["label"], plan["unit"], plan["tiles"], plan["depth"], plan["clamped"], plan["key"], *([integrals] * GROUP), *first,
    )


def fetch(buffers, source, row, v, c, held, sem, start):
    width = held.shape[0]
    for at in range(len(buffers)):

        @pl.when(source[v] == at)
        def _():
            rows = pl.ds(pl.multiple_of(row[v], width), width)
            copy = pltpu.make_async_copy(buffers[at].at[c, rows], held, sem)
            if start:
                copy.start()
            else:
                copy.wait()


def selection(slot, slots):
    width = slot.shape[-1]
    place = lax.broadcasted_iota(jnp.int32, (slots, width), 0)
    return (slot.reshape(1, width) == place).astype(jnp.float32).astype(jnp.bfloat16)


def add_kernel(nbuf, low, order, source, row, pieces, piece_from, piece_to, slot_ref, *refs):
    buffers = refs[:nbuf]
    out_ref, held, old, moved, sem, in_sem, out_sem = refs[-7:]
    shards = order.shape[0]
    step = pl.program_id(0)
    steps = pl.num_programs(0)
    nc = old.shape[0]
    slots = old.shape[1] * PIECE
    s = lax.rem(step, 2)

    def get(step, start):
        for c in range(nc):
            h = lax.rem(step, 2)
            fetch(buffers, source, row, order[low + step], c, held.at[h, c], sem.at[h, c], start)

    def each(v, c, do):
        for g in range(LABELS):
            size = pieces[g * shards + v]
            here = old.at[c, pl.ds(piece_from[g * shards + v], size)]
            there = out_ref.at[g, c, pl.ds(piece_to[g * shards + v], size)]

            @pl.when(size > 0)
            def _():
                do(g, here, there)

    v = order[low + step]

    @pl.when(step == 0)
    def _():
        get(step, True)

    @pl.when(step + 1 < steps)
    def _():
        get(step + 1, True)

    for c in range(nc):
        each(v, c, lambda g, here, there: pltpu.make_async_copy(there, here, in_sem.at[c, g]).start())
    onehot = selection(slot_ref[...], slots)
    get(step, False)
    for c in range(nc):
        sorted_rows = jnp.dot(onehot, held[s, c], preferred_element_type=jnp.float32)
        moved[...] = sorted_rows.astype(jnp.bfloat16).reshape(moved.shape)
        each(v, c, lambda g, here, there: pltpu.make_async_copy(there, here, in_sem.at[c, g]).wait())
        old[c] = old[c] + moved[...]
        each(v, c, lambda g, here, there: pltpu.make_async_copy(here, there, out_sem.at[c, g]).start())
    for c in range(nc):
        each(v, c, lambda g, here, there: pltpu.make_async_copy(here, there, out_sem.at[c, g]).wait())


def add_shards(ordered, buffers, places, low, high, plan, first=()):
    source, row, order = places
    nc, _, pairs = buffers[0].shape
    shards, _, shard = plan["slot"].shape
    slots = slots_of(shard)
    return pl.pallas_call(
        functools.partial(add_kernel, len(buffers), low),
        grid_spec=pltpu.PrefetchScalarGridSpec(
            num_scalar_prefetch=6,
            grid=(high - low,),
            in_specs=[
                pl.BlockSpec((1, 1, shard), lambda step, order, *_: (order[low + step], 0, 0))
            ]
            + [pl.BlockSpec(memory_space=pl.ANY)] * (len(buffers) + 1 + len(first)),
            out_specs=pl.BlockSpec(memory_space=pl.ANY),
            scratch_shapes=[
                pltpu.VMEM((2, nc, shard, pairs), jnp.bfloat16),
                pltpu.VMEM((nc, slots // PIECE, PIECE, pairs), jnp.bfloat16),
                pltpu.VMEM((slots // PIECE, PIECE, pairs), jnp.bfloat16),
                pltpu.SemaphoreType.DMA((2, nc)),
                pltpu.SemaphoreType.DMA((nc, LABELS)),
                pltpu.SemaphoreType.DMA((nc, LABELS)),
            ],
        ),
        out_shape=jax.ShapeDtypeStruct(ordered.shape, ordered.dtype),
        input_output_aliases={7 + len(buffers): 0},
        compiler_params=pltpu.CompilerParams(vmem_limit_bytes=VMEM),
        cost_estimate=COST,
        name="add_shards",
    )(
        order, source, row, plan["pieces"], plan["piece_from"], plan["piece_to"], plan["slot"], *buffers, ordered, *first,
    )


def multiply_kernel(low, high, span, label, unit, tiles, depth, label_end, label_turn, chunk, origin, *refs):
    count = 4 * (high - low)
    sources, amp_ref = refs[:count], refs[count]
    out_ref, total_ref, held, amp, held_sem, amp_sem = refs[-6:]
    step = pl.program_id(0)
    spare = label.shape[0] - 1
    i = place_of(span, step, spare)
    _, nc, rows, _ = sources[0].shape
    na = rows // RUN
    columns = total_ref.shape[0]
    count, deep = tiles[i], depth[i]
    slot, side = lax.rem(step, 2), lax.rem(label_turn[i], 2)
    follows = label_end[i]

    def get_units(step, start):
        j = place_of(span, step, spare)
        size, s = tiles[j] * depth[j], lax.rem(step, 2)
        for here in range(low, high):

            @pl.when(chunk[j] == here)
            def _():
                for at in range(4):
                    source = sources[4 * (here - low) + at]
                    copy = pltpu.make_async_copy(
                        source.at[pl.ds(unit[j], size)], held.at[s, at, pl.ds(0, size)], held_sem.at[s, at]
                    )
                    copy.start() if start else copy.wait()

    def get_amp(j, start):
        size, s = depth[j] * (TILE // PIECE), lax.rem(label_turn[j], 2)
        for c in range(nc):
            copy = pltpu.make_async_copy(
                amp_ref.at[label[j], c, pl.ds(0, size)], amp.at[s, c, pl.ds(0, size)], amp_sem.at[s, c]
            )
            copy.start() if start else copy.wait()

    active = span[0] + step < span[1]
    opens = active & ((step == 0) | (label[jnp.maximum(i - 1, 0)] != label[i]))

    @pl.when(active & (step == 0))
    def _():
        get_amp(i, True)
        get_units(step, True)

    @pl.when(span[0] + step + 1 < span[1])
    def _():
        get_units(step + 1, True)

    @pl.when(opens & (follows < span[1]))
    def _():
        get_amp(follows, True)

    @pl.when(active)
    def _():
        get_units(step, False)

    @pl.when(opens)
    def _():
        get_amp(i, False)

    def left(c, known):
        parts = []
        for s in range(4):
            for r in range(TILES):
                at = jnp.minimum(r, count - 1) * deep
                parts.append(jnp.concatenate([held[slot, s, at + k, c] for k in range(known)], axis=1))
        return jnp.concatenate(parts, axis=0)

    pieces, _, pairs = amp.shape[2:]
    for known in range(1, pieces * PIECE // TILE + 1):

        @pl.when(active & (deep == known))
        def _():
            lhs = jnp.concatenate([left(c, known) for c in range(nc)], axis=1)
            here = known * TILE // PIECE
            rhs = jnp.concatenate(
                [amp[side, c, :here].reshape(known * TILE, pairs) for c in range(nc)], axis=0
            )
            total = jnp.dot(lhs, rhs, preferred_element_type=jnp.float32)
            for j in range(columns):
                total_ref[j] = total[:, j * TILE : (j + 1) * TILE]

    @pl.when(active)
    def _():
        for s in range(4):
            for a in range(na):
                for j in range(columns):
                    picked = total_ref[j, pl.ds(s * TILES * rows + a, GROUP, stride=na), :]
                    out_ref[(origin[0] ^ s) * na + a, 0, :, j * TILE : (j + 1) * TILE] = (
                        picked.astype(jnp.bfloat16)
                    )


def multiply(sources, amplitudes, plan, origin, span, low, high, steps, done):
    _, nc, rows, _ = sources[0].shape
    _, _, pieces, piece, pairs = amplitudes.shape
    na = rows // RUN
    window = TILES * pieces * piece // TILE
    most = plan["label"].shape[0]
    spare = most - 1
    out_spec = pl.BlockSpec(
        (4 * na, 1, GROUP, pairs), lambda step, span, *_: (0, place_of(span, step, spare), 0, 0)
    )
    extra = [] if done is None else [done]
    return pl.pallas_call(
        functools.partial(multiply_kernel, low, high),
        grid_spec=pltpu.PrefetchScalarGridSpec(
            num_scalar_prefetch=9,
            grid=(steps,),
            in_specs=[pl.BlockSpec(memory_space=pl.ANY)] * (len(sources) + 1 + len(extra)),
            out_specs=out_spec,
            scratch_shapes=[
                pltpu.VMEM((pairs // TILE, 4 * TILES * rows, TILE), jnp.float32),
                pltpu.VMEM((2, 4, window, nc, rows, TILE), jnp.bfloat16),
                pltpu.VMEM((2, nc, pieces, piece, pairs), jnp.bfloat16),
                pltpu.SemaphoreType.DMA((2, 4)),
                pltpu.SemaphoreType.DMA((2, nc)),
            ],
        ),
        out_shape=jax.ShapeDtypeStruct((4 * na, most, GROUP, pairs), jnp.bfloat16),
        input_output_aliases={10 + len(sources): 0} if extra else {},
        compiler_params=pltpu.CompilerParams(vmem_limit_bytes=VMEM),
        cost_estimate=COST,
        name="multiply",
    )(
        span, plan["label"], plan["unit"],
        plan["tiles"], plan["depth"], plan["label_end"], plan["label_turn"], plan["chunk"], origin,
        *sources, amplitudes, *extra,
    )


def restore_kernel(live, orbital_ref, in_ref, out_ref, onehot, held):
    slots = orbital_ref.shape[1]
    rows, pairs = out_ref.shape[1:]

    @pl.when(pl.program_id(0) == 0)
    def _():
        place = lax.broadcasted_iota(jnp.int32, (rows, slots), 0)
        onehot[...] = (orbital_ref[...] == place).astype(jnp.float32).astype(jnp.bfloat16)

    sure = rows // GROUP
    for a in range(in_ref.shape[0]):
        for g in range(sure, in_ref.shape[1]):
            kept = jnp.where(g < live[0], in_ref[a, g], jnp.zeros_like(in_ref[a, g]))
            held[a, (g - sure) * GROUP : (g - sure + 1) * GROUP] = kept
        every = jnp.concatenate([in_ref[a, :sure].reshape(rows, pairs), held[a]], axis=0)
        out_ref[a] = jnp.dot(onehot[...], every, preferred_element_type=jnp.float32).astype(jnp.bfloat16)


def restore(grouped, plan, rows):
    block_a, most, _, pairs = grouped.shape
    return pl.pallas_call(
        restore_kernel,
        grid_spec=pltpu.PrefetchScalarGridSpec(
            num_scalar_prefetch=1,
            grid=(block_a // 4,),
            in_specs=[
                pl.BlockSpec((1, most * GROUP), lambda a, *_: (0, 0)),
                pl.BlockSpec((4, most, GROUP, pairs), lambda a, *_: (a, 0, 0, 0)),
            ],
            out_specs=pl.BlockSpec((4, rows, pairs), lambda a, *_: (a, 0, 0)),
            scratch_shapes=[
                pltpu.VMEM((rows, most * GROUP), jnp.bfloat16),
                pltpu.VMEM((4, (most - rows // GROUP) * GROUP, pairs), jnp.bfloat16),
            ],
        ),
        out_shape=jax.ShapeDtypeStruct((block_a, rows, pairs), jnp.bfloat16),
        compiler_params=pltpu.CompilerParams(vmem_limit_bytes=VMEM),
        cost_estimate=COST,
        name="restore",
    )(plan["starts"][-1:], plan["orbital"], grouped)


ORDER = (
    ((-1, 1), (1, 1), (1, 1), (1, 1)),
    ((-1, 2), (-1, 1), (-1, 1), (1, 2)),
    ((-1, 3), (-1, 2), (1, 2), (1, 3)),
)


class Gather:
    def __init__(self, amplitudes, vir, count):
        self.vir, self.count, self.lines = vir, count, count // 2
        self.ups, self.downs, self.across, self.sent = [amplitudes], [amplitudes], [], []

    def step(self, k, tied):
        count, lines, line = self.count, self.lines, self.vir // 2
        new = []
        if k == 0:
            send = self.ups[0]
        else:
            picks = ORDER[k - 1]
            send = self.pick(line, picks)
        if k > 0:
            send = tied(send)
        self.across.append(lax.ppermute(send, "vir", [(i, i ^ 1) for i in range(count)]))
        new.append(self.across[-1])
        if k < lines - 1:
            if k > 0:
                self.ups[k], self.downs[k] = tied(self.ups[k]), tied(self.downs[k])
            up, down = self.ups[k], self.downs[k]
            self.ups.append(lax.ppermute(up, "vir", [(i, i + 2) for i in range(2 * k, count - 2)]))
            self.downs.append(lax.ppermute(down, "vir", [(i, i - 2) for i in range(2, count - 2 * k)]))
            new += [self.ups[-1], self.downs[-1]]
        return new

    def pick(self, line, picks):
        kinds = [self.ups[hop] if way > 0 else self.downs[hop] for way, hop in picks]
        chosen = kinds[0]
        for at in range(1, self.lines):
            if kinds[at] is not kinds[at - 1]:
                chosen = jnp.where(line >= at, kinds[at], chosen)
        return chosen

    def places(self):
        lines, line, count = self.lines, self.vir // 2, self.count
        shards = jnp.arange(count, dtype=jnp.int32)
        ahead = shards // 2 - line
        same = jnp.where(ahead == 0, 0, jnp.where(ahead < 0, -ahead, lines - 1 + ahead))
        turn = jnp.zeros_like(shards)
        for k, picks in enumerate(ORDER):
            for at, (way, hop) in enumerate(picks):
                turn = jnp.where((line == at) & (ahead == -way * hop), k + 1, turn)
        own = shards % 2 == self.vir % 2
        source = jnp.where(own, same, 2 * lines - 1 + turn).astype(jnp.int32)
        step = jnp.where(own, jnp.abs(ahead), turn + 1) * count + shards
        place = jnp.sum((step[:, None] > step[None, :]).astype(jnp.int32), axis=1)
        order = jnp.sum(jnp.where(place[:, None] == shards[None, :], shards[:, None], 0), axis=0)
        return source, jnp.zeros((count,), jnp.int32), order.astype(jnp.int32)

    def buffers(self, k):
        hops = min(k, self.lines - 1)
        blank = [self.ups[0]] * (self.lines - 1 - hops)
        ways = self.ups[: hops + 1] + blank + self.downs[1 : hops + 1] + blank
        return ways + self.across[:k] + [self.ups[0]] * (self.lines - k)


class GatherWhole:
    def __init__(self, amplitudes):
        self.whole = lax.all_gather(amplitudes, "vir", axis=1, tiled=True)

    def step(self, k, tied):
        return []

    def places(self):
        shards = jnp.arange(8, dtype=jnp.int32)
        return jnp.zeros_like(shards), shards * (self.whole.shape[1] // 8), shards

    def buffers(self, k):
        return [self.whole]


def on_device(vir_count, integrals, amplitudes, irrep_labels):
    rows = integrals.shape[1]
    total = irrep_labels.shape[0]
    deepest = -(-(total // 4) // TILE)
    vir, occ = lax.axis_index("vir"), lax.axis_index("occ")
    plan = make_plan(irrep_labels, rows, vir, total // 8)
    most = ((rows // RUN + LABELS) * deepest, rows // GROUP + LABELS)
    core = [(i, i ^ 1) for i in range(4)]
    chip = [(i, i ^ 2) for i in range(4)]

    gather = Gather(amplitudes, vir, vir_count) if vir_count == 8 else GatherWhole(amplitudes)
    pairs = -(-deepest // 2)
    last = len(CHUNKS) - 1
    units, near, far, corner = [], [], [], []
    marks = [None]
    places = gather.places()
    pieces = deepest * TILE // PIECE
    ordered = jnp.zeros(
        (LABELS, amplitudes.shape[0], pieces, PIECE, amplitudes.shape[2]), jnp.bfloat16
    )
    come = (0, 1, 1, 7, 8)

    def tied(array):
        return after(array, marks[-1])

    def packed(at):
        span = plan["starts"][at : at + 2]
        return compact(integrals, plan, span, *CHUNKS[at], pairs, marks[-1:] if at > 1 else [])

    def exchange(at, units):
        return lax.ppermute(units, "occ", chip), lax.ppermute(units, "occ", core)

    units.append(packed(0))
    for k in range(last):
        new = gather.step(k, tied)
        if k > 0:
            units[k] = tied(units[k])
        ahead, beside = exchange(k, units[k])
        far.append(ahead)
        near.append(beside)
        if k > 0:
            far[k - 1] = after(far[k - 1], token(beside, marks[-1]))
            corner.append(lax.ppermute(far[k - 1], "occ", core))
            new.append(corner[-1])
        units.append(packed(k + 1))
        if k > 0 and come[k] > come[k - 1]:
            ordered = add_shards(
                ordered, gather.buffers(k), places, come[k - 1], come[k], plan, (marks[-1], units[-1])
            )
            new.append(ordered)
        marks.append(token(*new, ahead, beside, units[-1]))

    origin = occ.astype(jnp.int32).reshape(1)
    before = gather.buffers(last)
    gather.step(last, tied)
    ahead, beside = exchange(last, units[last])
    far.append(ahead)
    near.append(beside)
    corner.append(lax.ppermute(far[last - 1], "occ", core))
    ordered = add_shards(ordered, before, places, come[last - 1], come[last], plan)

    def more(*buffers):
        own = compact(integrals, plan, plan["starts"][last + 1 :], *most, pairs, [])
        ahead, beside = exchange(last + 1, own)
        return own, beside, ahead, lax.ppermute(ahead, "occ", core)

    shape = (most[0], *units[0].shape[1:])
    extra = unset(shape, token(ordered)), unset(shape), unset(shape), unset(shape)
    extra = lax.cond(plan["overflow"], more, lambda *buffers: buffers, *extra)
    ordered = add_shards(ordered, gather.buffers(last + 1), places, come[last], come[last + 1], plan)
    sources = [one for at in range(last) for one in (units[at], near[at], far[at], corner[at])]
    steps = min(sum(steps for _, steps in CHUNKS[:last]), rows // GROUP + LABELS)
    done = multiply(sources, ordered, plan, origin, plan["head"], 0, last, steps, None)
    far[last] = after(far[last], token(done))
    corner.append(lax.ppermute(far[last], "occ", core))
    sources = (units[last], near[last], far[last], corner[last], *extra)
    done = multiply(sources, ordered, plan, origin, plan["tail"], last, last + 2, most[1], done)
    return restore(done, plan, rows)


def solution(mesh):
    in_specs = (P("occ", "vir", None, None), P(None, "vir", "occ"), P())
    out_specs = P(None, "vir", "occ")
    return jax.shard_map(
        functools.partial(on_device, mesh.shape["vir"]),
        mesh=mesh, in_specs=in_specs, out_specs=out_specs, check_vma=False,
    )
```

```python
import functools

import jax
import jax.numpy as jnp
from jax import lax
from jax.experimental import pallas as pl
from jax.experimental.pallas import tpu as pltpu
from jax.sharding import PartitionSpec as P

LABELS = 8
TILE = 128
RUN = 4
TILES = 4
GROUP = RUN * TILES
PIECE = 16
STRIDE = 1024
VMEM = 56 * 2**20
COST = pl.CostEstimate(flops=10**6, bytes_accessed=10**6, transcendentals=0)
CHUNKS = ((40, 4), (104, 10), (112, 11), (192, 20))


def before(values):
    count = values.shape[0]
    earlier = jnp.arange(count)[:, None] > jnp.arange(count)[None, :]
    earlier = earlier.reshape(earlier.shape + (1,) * (values.ndim - 1))
    return jnp.sum(jnp.where(earlier, values[None], 0), axis=1)


def slots_of(shard):
    return -(-(shard + LABELS * 2 * (PIECE - 1)) // TILE) * TILE


def make_plan(labels, rows, vir, shard):
    total = labels.shape[0]
    blocks = total // TILE
    names = jnp.arange(LABELS)
    member = labels.reshape(1, blocks, TILE) == names[:, None, None]
    lower = jnp.arange(TILE)[:, None] < jnp.arange(TILE)[None, :]
    within = jnp.dot(
        member.astype(jnp.bfloat16).reshape(LABELS * blocks, TILE),
        lower.astype(jnp.bfloat16),
        preferred_element_type=jnp.float32,
    )
    within = within.reshape(LABELS, blocks, TILE).astype(jnp.int32)
    held = jnp.sum(member.astype(jnp.int32), axis=2)
    held_before = before(held.T).T
    rank = jnp.sum(jnp.where(member, within + held_before[:, :, None], 0), axis=0).reshape(total)
    sizes = jnp.sum(held, axis=1)
    depth = (sizes + TILE - 1) // TILE

    shards = total // shard
    part = jnp.sum(held.reshape(LABELS, shards, shard // TILE), axis=2)
    part_before = before(part.T).T
    pieces = jnp.where(part > 0, (part_before % PIECE + part + PIECE - 1) // PIECE, 0)
    piece_from = before(pieces)
    piece_to = part_before // PIECE
    move = PIECE * (piece_from - piece_to)
    slot = rank.reshape(shards, shard) + jnp.sum(
        jnp.where(member.reshape(LABELS, shards, shard), move[:, :, None], 0), axis=0
    )

    slices = total // rows
    mine = labels.reshape(1, slices, rows) == names[:, None, None]
    count = jnp.sum(mine.astype(jnp.int32), axis=2)
    row_tiles = (count + RUN - 1) // RUN
    groups = (count + GROUP - 1) // GROUP
    group_from = before(groups)
    unit_from = before(row_tiles * depth[:, None])
    most = rows // GROUP + LABELS + 1
    at = jnp.arange(most)[None, :, None]
    inside = (at >= group_from[:, None]) & (at < (group_from + groups)[:, None])

    def pick(values):
        return jnp.sum(jnp.where(inside, values, 0), axis=0)

    order = jnp.where(inside, at - group_from[:, None], 0)
    group_tiles = pick(jnp.clip(row_tiles[:, None] - TILES * order, 0, TILES))
    group_depth = pick(depth[:, None, None])
    group_unit = pick(unit_from[:, None] + order * TILES * depth[:, None, None])
    group_label = pick(names[:, None, None])
    label_end = pick((group_from + groups)[:, None])
    label_turn = pick(jnp.cumsum((groups > 0).astype(jnp.int32), axis=0)[:, None])
    group_end = group_unit + group_tiles * group_depth
    live = jnp.sum(groups, axis=0)
    valid = jnp.arange(most)[:, None] < live[None]
    starts, bases = [jnp.zeros_like(live)], [jnp.zeros_like(live)]
    for size, steps in CHUNKS:
        fits = valid & (group_end <= (bases[-1] + size)[None])
        fits = fits & (jnp.arange(most)[:, None] < (starts[-1] + steps)[None])
        starts.append(jnp.sum(fits.astype(jnp.int32), axis=0))
        bases.append(jnp.max(jnp.where(fits, group_end, 0), axis=0))
    overflow = jnp.max(live - starts[-1]) > 0
    starts.append(live)
    starts, bases = jnp.stack(starts), jnp.stack(bases)
    chunk = jnp.sum((jnp.arange(most)[:, None, None] >= starts[None, 1:-1]).astype(jnp.int32), axis=1)
    base = jnp.sum(
        jnp.where(chunk[None] == jnp.arange(len(CHUNKS) + 1)[:, None, None], bases[:, None], 0), axis=0
    )

    def own(values):
        return lax.dynamic_index_in_dim(values, vir, axis=values.ndim - 1, keepdims=False)

    group_from, count_before = own(group_from), own(before(count.T).T)
    row_label = lax.dynamic_slice_in_dim(labels, vir * rows, rows, 0)
    row_rank = lax.dynamic_slice_in_dim(rank, vir * rows, rows, 0)
    row_member = row_label[None, :] == names[:, None]
    row_slot = row_rank + jnp.sum(
        jnp.where(row_member, (GROUP * group_from - count_before)[:, None], 0), axis=0
    )
    hit = jnp.arange(most * GROUP)[:, None] == row_slot[None, :]
    orbital = jnp.sum(jnp.where(hit, jnp.arange(rows)[None, :] + 1, 0), axis=1) - 1
    return dict(
        key=(labels * STRIDE + rank).reshape(1, total),
        pieces=pieces.reshape(-1),
        piece_from=piece_from.reshape(-1),
        piece_to=piece_to.reshape(-1),
        slot=slot.reshape(shards, 1, shard),
        label=own(group_label),
        tiles=own(group_tiles),
        depth=own(group_depth),
        unit=own(group_unit - base),
        chunk=own(chunk),
        label_end=own(label_end),
        label_turn=own(label_turn),
        starts=own(starts),
        head=own(jnp.stack([starts[0], starts[-3]])),
        tail=own(jnp.stack([starts[-3], starts[-1]])),
        clamped=jnp.maximum(orbital, 0),
        orbital=orbital.reshape(1, most * GROUP),
        overflow=overflow,
    )


def place_of(span, step, spare):
    return jnp.where(span[1] > span[0], jnp.minimum(span[0] + step, span[1] - 1), spare)


def compact_kernel(span, label, unit, tiles, depth, orbital, key_ref, *refs):
    slabs = refs[:GROUP]
    out_ref, onehot, held, product, stage, sem = refs[-6:]
    step = pl.program_id(0)
    last = pl.num_programs(0) - 1
    i = place_of(span, step, label.shape[0] - 1)
    na, _, nc, width = slabs[0].shape
    rows = na * nc
    slot = lax.rem(step, 2)
    deep, name = depth[i], label[i]

    def active(step):
        return span[0] + step < span[1]

    @pl.when(active(step) & ((step == 0) | (label[jnp.maximum(i - 1, 0)] != name)))
    def _():
        def build(k, carry):
            place = lax.broadcasted_iota(jnp.int32, (2 * TILE, width), 0)
            place = place + (name * STRIDE + k * 2 * TILE)
            onehot[k] = (key_ref[...] == place).astype(jnp.float32).astype(jnp.bfloat16)
            return carry

        lax.fori_loop(0, (deep + 1) // 2, build, 0)

    def copy(step, s):
        j = place_of(span, step, label.shape[0] - 1)
        size = tiles[j] * depth[j]
        return pltpu.make_async_copy(
            stage.at[s, pl.ds(0, size)], out_ref.at[pl.ds(unit[j], size)], sem.at[s]
        )

    @pl.when((step >= 2) & active(step - 2))
    def _():
        copy(step - 2, slot).wait()

    @pl.when(active(step))
    def _():
        for r in range(GROUP):
            held[r * rows : (r + 1) * rows, :] = slabs[r][...].reshape(rows, width)

        def part(k, carry):
            full = lax.dot_general(
                held[...], onehot[k], (((1,), (1,)), ((), ())), preferred_element_type=jnp.float32
            )
            for h in range(2):
                product[h] = full[:, h * TILE : (h + 1) * TILE]
            for h in range(2):

                @pl.when(2 * k + h < deep)
                def _():
                    for c in range(nc):
                        one = product[h, pl.ds(c, GROUP * na, stride=nc), :].astype(jnp.bfloat16)
                        for r in range(TILES):
                            stage[slot, r * deep + 2 * k + h, c] = one[
                                r * RUN * na : (r + 1) * RUN * na
                            ]

            return carry

        lax.fori_loop(0, (deep + 1) // 2, part, 0)
        copy(step, slot).start()

    @pl.when((step == last) & (step >= 1) & active(step - 1))
    def _():
        copy(step - 1, 1 - slot).wait()

    @pl.when((step == last) & active(step))
    def _():
        copy(step, slot).wait()


def token(*arrays):
    def kernel(*refs):
        refs[-1][...] = jnp.zeros_like(refs[-1])

    return pl.pallas_call(
        kernel,
        in_specs=[pl.BlockSpec(memory_space=pl.ANY)] * len(arrays),
        out_shape=jax.ShapeDtypeStruct((8, TILE), jnp.float32),
        cost_estimate=COST,
        name="token",
    )(*arrays)


def unset(shape, *marks):
    def kernel(*refs):
        del refs

    return pl.pallas_call(
        kernel,
        in_specs=[pl.BlockSpec(memory_space=pl.ANY)] * len(marks),
        out_specs=pl.BlockSpec(memory_space=pl.ANY),
        out_shape=jax.ShapeDtypeStruct(shape, jnp.bfloat16),
        cost_estimate=COST,
        name="unset",
    )(*marks)


def after(array, mark):
    def kernel(*refs):
        del refs

    return pl.pallas_call(
        kernel,
        in_specs=[pl.BlockSpec(memory_space=pl.ANY)] * 2,
        out_specs=pl.BlockSpec(memory_space=pl.ANY),
        out_shape=jax.ShapeDtypeStruct(array.shape, array.dtype),
        input_output_aliases={0: 0},
        cost_estimate=COST,
        name="after",
    )(array, mark)


def compact(integrals, plan, span, size, steps, pairs, first):
    na, rows, nc, width = integrals.shape
    spare = plan["label"].shape[0] - 1

    def slab(r):
        def at(step, span, label, unit, tiles, depth, orbital):
            return 0, orbital[place_of(span, step, spare) * GROUP + r], 0, 0

        return pl.BlockSpec((na, 1, nc, width), at)

    return pl.pallas_call(
        compact_kernel,
        grid_spec=pltpu.PrefetchScalarGridSpec(
            num_scalar_prefetch=6,
            grid=(steps,),
            in_specs=[pl.BlockSpec((1, width), lambda step, *_: (0, 0))]
            + [slab(r) for r in range(GROUP)]
            + [pl.BlockSpec(memory_space=pl.ANY)] * len(first),
            out_specs=pl.BlockSpec(memory_space=pl.ANY),
            scratch_shapes=[
                pltpu.VMEM((pairs, 2 * TILE, width), jnp.bfloat16),
                pltpu.VMEM((GROUP * na * nc, width), jnp.bfloat16),
                pltpu.VMEM((2, GROUP * na * nc, TILE), jnp.float32),
                pltpu.VMEM((2, TILES * 2 * pairs, nc, RUN * na, TILE), jnp.bfloat16),
                pltpu.SemaphoreType.DMA((2,)),
            ],
        ),
        out_shape=jax.ShapeDtypeStruct((size, nc, RUN * na, TILE), jnp.bfloat16),
        compiler_params=pltpu.CompilerParams(vmem_limit_bytes=VMEM),
        cost_estimate=COST,
        name="compact",
    )(
        span, plan["label"], plan["unit"], plan["tiles"], plan["depth"], plan["clamped"], plan["key"], *([integrals] * GROUP), *first,
    )


def fetch(buffers, source, row, v, c, held, sem, start):
    width = held.shape[0]
    for at in range(len(buffers)):

        @pl.when(source[v] == at)
        def _():
            rows = pl.ds(pl.multiple_of(row[v], width), width)
            copy = pltpu.make_async_copy(buffers[at].at[c, rows], held, sem)
            if start:
                copy.start()
            else:
                copy.wait()


def selection(slot, slots):
    width = slot.shape[-1]
    place = lax.broadcasted_iota(jnp.int32, (slots, width), 0)
    return (slot.reshape(1, width) == place).astype(jnp.float32).astype(jnp.bfloat16)


def add_kernel(nbuf, low, order, source, row, pieces, piece_from, piece_to, slot_ref, *refs):
    buffers = refs[:nbuf]
    out_ref, held, old, moved, sem, in_sem, out_sem = refs[-7:]
    shards = order.shape[0]
    step = pl.program_id(0)
    steps = pl.num_programs(0)
    nc = old.shape[0]
    slots = old.shape[1] * PIECE
    s = lax.rem(step, 2)

    def get(step, start):
        for c in range(nc):
            h = lax.rem(step, 2)
            fetch(buffers, source, row, order[low + step], c, held.at[h, c], sem.at[h, c], start)

    def each(v, c, do):
        for g in range(LABELS):
            size = pieces[g * shards + v]
            here = old.at[c, pl.ds(piece_from[g * shards + v], size)]
            there = out_ref.at[g, c, pl.ds(piece_to[g * shards + v], size)]

            @pl.when(size > 0)
            def _():
                do(g, here, there)

    v = order[low + step]

    @pl.when(step == 0)
    def _():
        get(step, True)

    @pl.when(step + 1 < steps)
    def _():
        get(step + 1, True)

    for c in range(nc):
        each(v, c, lambda g, here, there: pltpu.make_async_copy(there, here, in_sem.at[c, g]).start())
    onehot = selection(slot_ref[...], slots)
    get(step, False)
    for c in range(nc):
        sorted_rows = jnp.dot(onehot, held[s, c], preferred_element_type=jnp.float32)
        moved[...] = sorted_rows.astype(jnp.bfloat16).reshape(moved.shape)
        each(v, c, lambda g, here, there: pltpu.make_async_copy(there, here, in_sem.at[c, g]).wait())
        old[c] = old[c] + moved[...]
        each(v, c, lambda g, here, there: pltpu.make_async_copy(here, there, out_sem.at[c, g]).start())
    for c in range(nc):
        each(v, c, lambda g, here, there: pltpu.make_async_copy(here, there, out_sem.at[c, g]).wait())


def add_shards(ordered, buffers, places, low, high, plan, first=()):
    source, row, order = places
    nc, _, pairs = buffers[0].shape
    shards, _, shard = plan["slot"].shape
    slots = slots_of(shard)
    return pl.pallas_call(
        functools.partial(add_kernel, len(buffers), low),
        grid_spec=pltpu.PrefetchScalarGridSpec(
            num_scalar_prefetch=6,
            grid=(high - low,),
            in_specs=[
                pl.BlockSpec((1, 1, shard), lambda step, order, *_: (order[low + step], 0, 0))
            ]
            + [pl.BlockSpec(memory_space=pl.ANY)] * (len(buffers) + 1 + len(first)),
            out_specs=pl.BlockSpec(memory_space=pl.ANY),
            scratch_shapes=[
                pltpu.VMEM((2, nc, shard, pairs), jnp.bfloat16),
                pltpu.VMEM((nc, slots // PIECE, PIECE, pairs), jnp.bfloat16),
                pltpu.VMEM((slots // PIECE, PIECE, pairs), jnp.bfloat16),
                pltpu.SemaphoreType.DMA((2, nc)),
                pltpu.SemaphoreType.DMA((nc, LABELS)),
                pltpu.SemaphoreType.DMA((nc, LABELS)),
            ],
        ),
        out_shape=jax.ShapeDtypeStruct(ordered.shape, ordered.dtype),
        input_output_aliases={7 + len(buffers): 0},
        compiler_params=pltpu.CompilerParams(vmem_limit_bytes=VMEM),
        cost_estimate=COST,
        name="add_shards",
    )(
        order, source, row, plan["pieces"], plan["piece_from"], plan["piece_to"], plan["slot"], *buffers, ordered, *first,
    )


def multiply_kernel(low, high, span, label, unit, tiles, depth, label_end, label_turn, chunk, origin, *refs):
    count = 4 * (high - low)
    sources, amp_ref = refs[:count], refs[count]
    out_ref, total_ref, held, amp, held_sem, amp_sem = refs[-6:]
    step = pl.program_id(0)
    spare = label.shape[0] - 1
    i = place_of(span, step, spare)
    _, nc, rows, _ = sources[0].shape
    na = rows // RUN
    columns = total_ref.shape[0]
    count, deep = tiles[i], depth[i]
    slot, side = lax.rem(step, 2), lax.rem(label_turn[i], 2)
    follows = label_end[i]

    def get_units(step, start):
        j = place_of(span, step, spare)
        size, s = tiles[j] * depth[j], lax.rem(step, 2)
        for here in range(low, high):

            @pl.when(chunk[j] == here)
            def _():
                for at in range(4):
                    source = sources[4 * (here - low) + at]
                    copy = pltpu.make_async_copy(
                        source.at[pl.ds(unit[j], size)], held.at[s, at, pl.ds(0, size)], held_sem.at[s, at]
                    )
                    copy.start() if start else copy.wait()

    def get_amp(j, start):
        size, s = depth[j] * (TILE // PIECE), lax.rem(label_turn[j], 2)
        for c in range(nc):
            copy = pltpu.make_async_copy(
                amp_ref.at[label[j], c, pl.ds(0, size)], amp.at[s, c, pl.ds(0, size)], amp_sem.at[s, c]
            )
            copy.start() if start else copy.wait()

    active = span[0] + step < span[1]
    opens = active & ((step == 0) | (label[jnp.maximum(i - 1, 0)] != label[i]))

    @pl.when(active & (step == 0))
    def _():
        get_amp(i, True)
        get_units(step, True)

    @pl.when(span[0] + step + 1 < span[1])
    def _():
        get_units(step + 1, True)

    @pl.when(opens & (follows < span[1]))
    def _():
        get_amp(follows, True)

    @pl.when(active)
    def _():
        get_units(step, False)

    @pl.when(opens)
    def _():
        get_amp(i, False)

    def left(c, known):
        parts = []
        for s in range(4):
            for r in range(TILES):
                at = jnp.minimum(r, count - 1) * deep
                parts.append(jnp.concatenate([held[slot, s, at + k, c] for k in range(known)], axis=1))
        return jnp.concatenate(parts, axis=0)

    pieces, _, pairs = amp.shape[2:]
    for known in range(1, pieces * PIECE // TILE + 1):

        @pl.when(active & (deep == known))
        def _():
            lhs = jnp.concatenate([left(c, known) for c in range(nc)], axis=1)
            here = known * TILE // PIECE
            rhs = jnp.concatenate(
                [amp[side, c, :here].reshape(known * TILE, pairs) for c in range(nc)], axis=0
            )
            total = jnp.dot(lhs, rhs, preferred_element_type=jnp.float32)
            for j in range(columns):
                total_ref[j] = total[:, j * TILE : (j + 1) * TILE]

    @pl.when(active)
    def _():
        for s in range(4):
            for a in range(na):
                for j in range(columns):
                    picked = total_ref[j, pl.ds(s * TILES * rows + a, GROUP, stride=na), :]
                    out_ref[(origin[0] ^ s) * na + a, 0, :, j * TILE : (j + 1) * TILE] = (
                        picked.astype(jnp.bfloat16)
                    )


def multiply(sources, amplitudes, plan, origin, span, low, high, steps, done):
    _, nc, rows, _ = sources[0].shape
    _, _, pieces, piece, pairs = amplitudes.shape
    na = rows // RUN
    window = TILES * pieces * piece // TILE
    most = plan["label"].shape[0]
    spare = most - 1
    out_spec = pl.BlockSpec(
        (4 * na, 1, GROUP, pairs), lambda step, span, *_: (0, place_of(span, step, spare), 0, 0)
    )
    extra = [] if done is None else [done]
    return pl.pallas_call(
        functools.partial(multiply_kernel, low, high),
        grid_spec=pltpu.PrefetchScalarGridSpec(
            num_scalar_prefetch=9,
            grid=(steps,),
            in_specs=[pl.BlockSpec(memory_space=pl.ANY)] * (len(sources) + 1 + len(extra)),
            out_specs=out_spec,
            scratch_shapes=[
                pltpu.VMEM((pairs // TILE, 4 * TILES * rows, TILE), jnp.float32),
                pltpu.VMEM((2, 4, window, nc, rows, TILE), jnp.bfloat16),
                pltpu.VMEM((2, nc, pieces, piece, pairs), jnp.bfloat16),
                pltpu.SemaphoreType.DMA((2, 4)),
                pltpu.SemaphoreType.DMA((2, nc)),
            ],
        ),
        out_shape=jax.ShapeDtypeStruct((4 * na, most, GROUP, pairs), jnp.bfloat16),
        input_output_aliases={10 + len(sources): 0} if extra else {},
        compiler_params=pltpu.CompilerParams(vmem_limit_bytes=VMEM),
        cost_estimate=COST,
        name="multiply",
    )(
        span, plan["label"], plan["unit"],
        plan["tiles"], plan["depth"], plan["label_end"], plan["label_turn"], plan["chunk"], origin,
        *sources, amplitudes, *extra,
    )


def restore_kernel(live, orbital_ref, in_ref, out_ref, onehot, held):
    slots = orbital_ref.shape[1]
    rows, pairs = out_ref.shape[1:]

    @pl.when(pl.program_id(0) == 0)
    def _():
        place = lax.broadcasted_iota(jnp.int32, (rows, slots), 0)
        onehot[...] = (orbital_ref[...] == place).astype(jnp.float32).astype(jnp.bfloat16)

    sure = rows // GROUP
    for a in range(in_ref.shape[0]):
        for g in range(sure, in_ref.shape[1]):
            kept = jnp.where(g < live[0], in_ref[a, g], jnp.zeros_like(in_ref[a, g]))
            held[a, (g - sure) * GROUP : (g - sure + 1) * GROUP] = kept
        every = jnp.concatenate([in_ref[a, :sure].reshape(rows, pairs), held[a]], axis=0)
        out_ref[a] = jnp.dot(onehot[...], every, preferred_element_type=jnp.float32).astype(jnp.bfloat16)


def restore(grouped, plan, rows):
    block_a, most, _, pairs = grouped.shape
    return pl.pallas_call(
        restore_kernel,
        grid_spec=pltpu.PrefetchScalarGridSpec(
            num_scalar_prefetch=1,
            grid=(block_a // 4,),
            in_specs=[
                pl.BlockSpec((1, most * GROUP), lambda a, *_: (0, 0)),
                pl.BlockSpec((4, most, GROUP, pairs), lambda a, *_: (a, 0, 0, 0)),
            ],
            out_specs=pl.BlockSpec((4, rows, pairs), lambda a, *_: (a, 0, 0)),
            scratch_shapes=[
                pltpu.VMEM((rows, most * GROUP), jnp.bfloat16),
                pltpu.VMEM((4, (most - rows // GROUP) * GROUP, pairs), jnp.bfloat16),
            ],
        ),
        out_shape=jax.ShapeDtypeStruct((block_a, rows, pairs), jnp.bfloat16),
        compiler_params=pltpu.CompilerParams(vmem_limit_bytes=VMEM),
        cost_estimate=COST,
        name="restore",
    )(plan["starts"][-1:], plan["orbital"], grouped)


ORDER = (
    ((-1, 1), (1, 1), (1, 1), (1, 1)),
    ((-1, 2), (-1, 1), (-1, 1), (1, 2)),
    ((-1, 3), (-1, 2), (1, 2), (1, 3)),
)


class Gather:
    def __init__(self, amplitudes, vir, count):
        self.vir, self.count, self.lines = vir, count, count // 2
        self.ups, self.downs, self.across, self.sent = [amplitudes], [amplitudes], [], []

    def step(self, k, tied):
        count, lines, line = self.count, self.lines, self.vir // 2
        new = []
        if k == 0:
            send = self.ups[0]
        else:
            picks = ORDER[k - 1]
            send = self.pick(line, picks)
        if k > 0:
            send = tied(send)
        self.across.append(lax.ppermute(send, "vir", [(i, i ^ 1) for i in range(count)]))
        new.append(self.across[-1])
        if k < lines - 1:
            if k > 0:
                self.ups[k], self.downs[k] = tied(self.ups[k]), tied(self.downs[k])
            up, down = self.ups[k], self.downs[k]
            self.ups.append(lax.ppermute(up, "vir", [(i, i + 2) for i in range(2 * k, count - 2)]))
            self.downs.append(lax.ppermute(down, "vir", [(i, i - 2) for i in range(2, count - 2 * k)]))
            new += [self.ups[-1], self.downs[-1]]
        return new

    def pick(self, line, picks):
        kinds = [self.ups[hop] if way > 0 else self.downs[hop] for way, hop in picks]
        chosen = kinds[0]
        for at in range(1, self.lines):
            if kinds[at] is not kinds[at - 1]:
                chosen = jnp.where(line >= at, kinds[at], chosen)
        return chosen

    def places(self):
        lines, line, count = self.lines, self.vir // 2, self.count
        shards = jnp.arange(count, dtype=jnp.int32)
        ahead = shards // 2 - line
        same = jnp.where(ahead == 0, 0, jnp.where(ahead < 0, -ahead, lines - 1 + ahead))
        turn = jnp.zeros_like(shards)
        for k, picks in enumerate(ORDER):
            for at, (way, hop) in enumerate(picks):
                turn = jnp.where((line == at) & (ahead == -way * hop), k + 1, turn)
        own = shards % 2 == self.vir % 2
        source = jnp.where(own, same, 2 * lines - 1 + turn).astype(jnp.int32)
        step = jnp.where(own, jnp.abs(ahead), turn + 1) * count + shards
        place = jnp.sum((step[:, None] > step[None, :]).astype(jnp.int32), axis=1)
        order = jnp.sum(jnp.where(place[:, None] == shards[None, :], shards[:, None], 0), axis=0)
        return source, jnp.zeros((count,), jnp.int32), order.astype(jnp.int32)

    def buffers(self, k):
        hops = min(k, self.lines - 1)
        blank = [self.ups[0]] * (self.lines - 1 - hops)
        ways = self.ups[: hops + 1] + blank + self.downs[1 : hops + 1] + blank
        return ways + self.across[:k] + [self.ups[0]] * (self.lines - k)


class GatherWhole:
    def __init__(self, amplitudes):
        self.whole = lax.all_gather(amplitudes, "vir", axis=1, tiled=True)

    def step(self, k, tied):
        return []

    def places(self):
        shards = jnp.arange(8, dtype=jnp.int32)
        return jnp.zeros_like(shards), shards * (self.whole.shape[1] // 8), shards

    def buffers(self, k):
        return [self.whole]


def on_device(vir_count, integrals, amplitudes, irrep_labels):
    rows = integrals.shape[1]
    total = irrep_labels.shape[0]
    deepest = -(-(total // 4) // TILE)
    vir, occ = lax.axis_index("vir"), lax.axis_index("occ")
    plan = make_plan(irrep_labels, rows, vir, total // 8)
    most = ((rows // RUN + LABELS) * deepest, rows // GROUP + LABELS)
    core = [(i, i ^ 1) for i in range(4)]
    chip = [(i, i ^ 2) for i in range(4)]

    gather = Gather(amplitudes, vir, vir_count) if vir_count == 8 else GatherWhole(amplitudes)
    pairs = -(-deepest // 2)
    last = len(CHUNKS) - 1
    units, near, far, corner = [], [], [], []
    marks = [None]
    places = gather.places()
    pieces = deepest * TILE // PIECE
    ordered = jnp.zeros(
        (LABELS, amplitudes.shape[0], pieces, PIECE, amplitudes.shape[2]), jnp.bfloat16
    )
    come = (0, 1, 1, 7, 8)

    def tied(array):
        return after(array, marks[-1])

    def packed(at):
        span = plan["starts"][at : at + 2]
        return compact(integrals, plan, span, *CHUNKS[at], pairs, marks[-1:] if at > 1 else [])

    def exchange(at, units):
        return lax.ppermute(units, "occ", chip), lax.ppermute(units, "occ", core)

    units.append(packed(0))
    for k in range(last):
        new = gather.step(k, tied)
        if k > 0:
            units[k] = tied(units[k])
        ahead, beside = exchange(k, units[k])
        far.append(ahead)
        near.append(beside)
        if k > 0:
            far[k - 1] = after(far[k - 1], token(beside, marks[-1]))
            corner.append(lax.ppermute(far[k - 1], "occ", core))
            new.append(corner[-1])
        units.append(packed(k + 1))
        if k > 0 and come[k] > come[k - 1]:
            ordered = add_shards(
                ordered, gather.buffers(k), places, come[k - 1], come[k], plan, (marks[-1], units[-1])
            )
            new.append(ordered)
        marks.append(token(*new, ahead, beside, units[-1]))

    origin = occ.astype(jnp.int32).reshape(1)
    before = gather.buffers(last)
    gather.step(last, tied)
    ahead, beside = exchange(last, units[last])
    far.append(ahead)
    near.append(beside)
    corner.append(lax.ppermute(far[last - 1], "occ", core))
    ordered = add_shards(ordered, before, places, come[last - 1], come[last], plan)

    def more(*buffers):
        own = compact(integrals, plan, plan["starts"][last + 1 :], *most, pairs, [])
        ahead, beside = exchange(last + 1, own)
        return own, beside, ahead, lax.ppermute(ahead, "occ", core)

    shape = (most[0], *units[0].shape[1:])
    extra = unset(shape, token(ordered)), unset(shape), unset(shape), unset(shape)
    extra = lax.cond(plan["overflow"], more, lambda *buffers: buffers, *extra)
    ordered = add_shards(ordered, gather.buffers(last + 1), places, come[last], come[last + 1], plan)
    sources = [one for at in range(last) for one in (units[at], near[at], far[at], corner[at])]
    steps = min(sum(steps for _, steps in CHUNKS[:last]), rows // GROUP + LABELS)
    done = multiply(sources, ordered, plan, origin, plan["head"], 0, last, steps, None)
    far[last] = after(far[last], token(done))
    corner.append(lax.ppermute(far[last], "occ", core))
    sources = (units[last], near[last], far[last], corner[last], *extra)
    done = multiply(sources, ordered, plan, origin, plan["tail"], last, last + 2, most[1], done)
    return restore(done, plan, rows)


def solution(mesh):
    in_specs = (P("occ", "vir", None, None), P(None, "vir", "occ"), P())
    out_specs = P(None, "vir", "occ")
    return jax.shard_map(
        functools.partial(on_device, mesh.shape["vir"]),
        mesh=mesh, in_specs=in_specs, out_specs=out_specs, check_vma=False,
    )
```
